256 devices in a mesh: dp: 4 (over x), fsdp: 64 (over y, z, core).
Axes of the slice: x: 4, y: 4, z: 8, core: 2. Of those that a mesh axis runs over, the one named last changes fastest.
Arguments:
- features: bfloat16 [32768, 1408], P(('dp', 'fsdp')), may hold values from -24 to 24
- w_first: bfloat16 [1408, 1408], P('fsdp'), may hold values from -0.15625 to 0.15625
- w_second: bfloat16 [1408, 256], P('fsdp'), may hold values from -0.15625 to 0.15625
- partner: int32 [32768], P(('dp', 'fsdp')), may hold values from 0 to 32767, as said below
Outputs:
- loss: float32 [], replicated
- grad_features: bfloat16 [32768, 1408], P(('dp', 'fsdp'))
- grad_first: float32 [1408, 1408], P('fsdp')
- grad_second: float32 [1408, 256], P('fsdp')
The draws below stay inside these ranges and needn't reach their ends.
Inputs may be any that keep to these rules, and one draw needn't show every extreme that they name: partner[partner[i]] == i and partner[i] != i: every row is paired with exactly one other row, and both lie in the same aligned block of 8192 rows.
All inputs are finite; a program needn't handle non-finite values.
Results may differ from the reference program's by a relative error of at most 0.025.
Values may be sent and summed in bfloat16 or wider, within the bound.
No kernel may reach another device: no remote copies, remote signals or barrier semaphores. Data moves between devices by JAX's collectives and lax.ppermute only.
A program may use at most 128 MiB of HBM per device.

```python
import jax
import jax.numpy as jnp
from jax import lax

D = 1408
HID = 1408
PD = 256
TOK_DEV = 128
BLOCK_ROWS = 8192
TOKENS = 32768


def shuffle_block(key_block):
    return jax.random.permutation(key_block, BLOCK_ROWS)


def pairing(key):
    blocks = TOKENS // BLOCK_ROWS
    keys = jax.random.split(jax.random.fold_in(key, 101), blocks)
    perms = jax.vmap(shuffle_block)(keys).astype(jnp.int32)
    offsets = (jnp.arange(blocks, dtype=jnp.int32) * BLOCK_ROWS)[:, None]
    placed = perms + offsets
    evens = placed[:, 0::2].reshape(-1)
    odds = placed[:, 1::2].reshape(-1)
    mates = jnp.zeros((TOKENS,), jnp.int32).at[evens].set(odds).at[odds].set(evens)
    images = jnp.arange(TOKENS // 2, dtype=jnp.int32)
    image_of = jnp.zeros((TOKENS,), jnp.int32).at[evens].set(images).at[odds].set(images)
    return (mates, image_of)


def draw_partner(key, part):
    mates, image_of = pairing(key)
    return mates


def draw_features(key, part):
    mates, image_of = pairing(key)
    key = jax.random.fold_in(key, 13)
    devices = TOKENS // TOK_DEV
    paired = max(devices // 2, 1)
    row_dev = jnp.arange(TOKENS, dtype=jnp.int32) // TOK_DEV
    place = row_dev % paired
    rise = (row_dev.astype(jnp.float32) / float(devices))[:, None]
    shared = jax.random.normal(jax.random.fold_in(key, 2), (paired, D), jnp.float32)
    faces = jax.random.normal(jax.random.fold_in(key, 3), (TOKENS // 2, D), jnp.float32)
    noise = jax.random.normal(jax.random.fold_in(key, 4), (TOKENS, D), jnp.float32)
    values = (0.6 + 0.9 * rise) * shared[place] + 0.7 * faces[image_of] + 0.3 * noise
    shards = BLOCK_ROWS // TOK_DEV
    width_piece = D // shards
    order = jax.random.permutation(jax.random.fold_in(key, 6), shards).astype(jnp.int32)
    row_shard = jnp.arange(TOKENS, dtype=jnp.int32) // TOK_DEV % shards
    col_piece = jnp.arange(D, dtype=jnp.int32) // width_piece
    boost = jnp.where(order[row_shard][:, None] == col_piece[None, :], 3.0, 1.0)
    values = jnp.clip(values * boost, -24.0, 24.0)
    return values.astype(jnp.bfloat16)


def shard_levels(rng, extent, cuts, least, top_value):
    level = 1.0
    for position, shards_of in cuts:
        draws = jax.random.uniform(jax.random.fold_in(jax.random.fold_in(rng, 6), position), (shards_of,), jnp.float32, least / len(cuts), top_value / len(cuts))
        level = level * jnp.repeat(jnp.exp(draws), extent[position] // shards_of).reshape((-1,) + (1,) * (len(extent) - 1 - position))
    return level


def scatter_about(stream_key, extent, deviation, bound, cuts=(), kind=jnp.bfloat16):
    values = deviation * jax.random.normal(stream_key, extent, jnp.float32)
    if cuts:
        values = values * shard_levels(stream_key, extent, cuts, -0.22, 0.18)
    return jnp.clip(values, -bound, bound).astype(kind)


def setup_inputs(seed: int = 0) -> dict:
    arg_keys = jax.random.split(jax.random.key(seed), 5)
    return {
        "features": draw_features(jax.random.fold_in(arg_keys[4], 71), 0),
        "w_first": scatter_about(arg_keys[1], (D, HID), D ** -0.5, 0.15625, ((0, 64),)),
        "w_second": scatter_about(arg_keys[2], (HID, PD), HID ** -0.5, 0.15625, ((0, 64),)),
        "partner": draw_partner(jax.random.fold_in(arg_keys[4], 71), 0),
    }


TEMPER = 0.1
EPSILON = 1e-06

def reference(features, w_first, w_second, partner):
    total = features.shape[0]
    pre = jnp.dot(features, w_first, preferred_element_type=jnp.float32)
    act = jnp.maximum(pre, 0.0).astype(jnp.bfloat16)
    proj = jnp.dot(act, w_second, preferred_element_type=jnp.float32)
    norm = jnp.sqrt(lax.optimization_barrier(jnp.sum(proj * proj, axis=1)) + EPSILON)
    unit = proj / norm[:, None]
    emb = unit.astype(jnp.bfloat16)
    block = 512 if total % 512 == 0 else total
    steps = total // block
    columns = jnp.arange(total, dtype=jnp.int32)

    def forward(index):
        start = (index * block).astype(jnp.int32)
        rows = lax.dynamic_slice_in_dim(emb, start, block, 0)
        sim = jnp.dot(rows, emb.T, preferred_element_type=jnp.float32) / TEMPER
        keep = (start + jnp.arange(block, dtype=jnp.int32))[:, None] != columns[None, :]
        terms = jnp.where(keep, jnp.exp(sim - 1.0 / TEMPER), 0.0)
        return jnp.log(lax.optimization_barrier(jnp.sum(terms, axis=1))) + 1.0 / TEMPER
    lse = lax.map(forward, jnp.arange(steps, dtype=jnp.int32)).reshape(total)
    mate = emb[partner].astype(jnp.float32)
    spos = lax.optimization_barrier(jnp.sum(emb.astype(jnp.float32) * mate, axis=1)) / TEMPER
    loss = jnp.sum(lse - spos) / total

    def backward(index):
        start = (index * block).astype(jnp.int32)
        rows = lax.dynamic_slice_in_dim(emb, start, block, 0)
        row_lse = lax.dynamic_slice_in_dim(lse, start, block, 0)
        sim = jnp.dot(rows, emb.T, preferred_element_type=jnp.float32) / TEMPER
        keep = (start + jnp.arange(block, dtype=jnp.int32))[:, None] != columns[None, :]
        weight = jnp.exp(sim - row_lse[:, None]) + jnp.exp(sim - lse[None, :])
        weight = jnp.where(keep, weight, 0.0).astype(jnp.bfloat16)
        return jnp.dot(weight, emb, preferred_element_type=jnp.float32)
    accum = lax.map(backward, jnp.arange(steps, dtype=jnp.int32)).reshape(total, emb.shape[1])
    grad_emb = (accum - 2.0 * mate) / TEMPER
    dproj = ((grad_emb - unit * lax.optimization_barrier(jnp.sum(unit * grad_emb, axis=1, keepdims=True))) / norm[:, None]).astype(jnp.bfloat16)
    dact = jnp.dot(dproj, w_second.T, preferred_element_type=jnp.float32)
    dpre = jnp.where(pre > 0.0, dact, 0.0).astype(jnp.bfloat16)
    grad_features = jnp.dot(dpre, w_first.T, preferred_element_type=jnp.float32).astype(jnp.bfloat16)
    scale = jnp.sqrt(jnp.float32(total))
    grad_first = jnp.dot(features.T, dpre, preferred_element_type=jnp.float32) / scale
    grad_second = jnp.dot(act.T, dproj, preferred_element_type=jnp.float32) / scale
    return (loss, grad_features, grad_first, grad_second)
```

```python
import jax
import jax.numpy as jnp
from jax import lax
from jax.sharding import PartitionSpec as P

TEMPER = 0.1
EPSILON = 1e-06
NX, NY, NZ, NC = 4, 4, 8, 2
BF = jnp.bfloat16
F32 = jnp.float32

ZSLOTS = [(1, 0, 0), (1, 0, 1)]
ZSLOTS += [(1, s, f) for s in (1, 2, 3) for f in (0, 1)] + [(1, 4, 0), (1, 4, 1)]
ZSLOTS += [(-1, s, f) for s in (1, 2, 3) for f in (1, 0)]


def fsdp_perm(place):
    pairs = []
    for y in range(NY):
        for z in range(NZ):
            for c in range(NC):
                y2, z2, c2 = place(y, z, c)
                pairs.append(((y * NZ + z) * NC + c, ((y2 % NY) * NZ + z2 % NZ) * NC + c2))
    return pairs


PERM_SWAP = fsdp_perm(lambda y, z, c: (y, z, 1 - c))
PERM_RING = fsdp_perm(lambda y, z, c: (y, z + 1 - 2 * c, c))
PERM_BACK = fsdp_perm(lambda y, z, c: (y, z - 1 + 2 * c, c))


def swap(v):
    return lax.ppermute(v, "fsdp", PERM_SWAP)


def ring(v):
    return lax.ppermute(v, "fsdp", PERM_RING)


def back(v):
    return lax.ppermute(v, "fsdp", PERM_BACK)


def move_y(v, by):
    return lax.ppermute(v, "fsdp", fsdp_perm(lambda y, z, c: (y + by, z, c)))


def move_z(v, by):
    return lax.ppermute(v, "fsdp", fsdp_perm(lambda y, z, c: (y, z + by, c)))


def move_x(v, by):
    return lax.ppermute(v, "dp", [(i, (i + by) % NX) for i in range(NX)])


def gather_y(v):
    return [v] + [move_y(v, k) for k in range(1, NY)]


def gather_x(v):
    return [v] + [move_x(v, k) for k in range(1, NX)]


def gather_zc(v):
    m = v.shape[0]
    block = jnp.concatenate([v, swap(v)], axis=0)
    one = ring(block)
    two = ring(one)
    three = ring(two)
    four = ring(three[:m])
    mine = jnp.concatenate([one, two, three, four], axis=0)
    other = swap(mine)
    return jnp.concatenate([block, mine, other[6 * m :], other[: 6 * m]], axis=0)


def scatter_zc(v):
    m = v.shape[0] // 16
    block, mine = v[: 2 * m], v[2 * m : 9 * m]
    other = jnp.concatenate([v[10 * m :], v[9 * m : 10 * m]], axis=0)
    mine = mine + swap(other)
    got = back(mine[6 * m :])
    three = mine[4 * m : 6 * m]
    got = back(jnp.concatenate([three[:m] + got, three[m:]], axis=0))
    got = back(mine[2 * m : 4 * m] + got)
    got = back(mine[: 2 * m] + got)
    block = block + got
    return block[:m] + swap(block[m:])


def total_z(v):
    low, high = move_z(v, 1), move_z(v, -1)
    part = v + low
    return part + high + move_z(part + high, 3) + move_z(part, -3)


def total_x(v):
    return sum(gather_x(v))


def total_y(v):
    return sum(gather_y(v))


def dot(a, b):
    return jnp.dot(a, b, preferred_element_type=F32)


def dot_nt(a, b):
    return lax.dot_general(a, b, (((1,), (1,)), ((), ())), preferred_element_type=F32)


def dot_tn(a, b):
    return lax.dot_general(a, b, (((0,), (0,)), ((), ())), preferred_element_type=F32)


def reorder(table, v):
    return jnp.sum(jnp.where(table[:, :, None], v[None], 0.0), axis=1)


def on_device(features, w_first, w_second, partner):
    rows, depth = features.shape
    hidden, width = w_second.shape[0] * NY * NZ * NC, w_second.shape[1]
    share = depth // (NY * NZ * NC)
    pad = -(-share // 8) * 8
    part = hidden // NX
    x = lax.axis_index("dp")
    f = lax.axis_index("fsdp")
    y, z, c = f // (NZ * NC), f // NC % NZ, f % NC
    step = 1 - 2 * c
    zslot = jnp.stack([(z - sign * dist * step) % NZ * NC + (c ^ flip) for sign, dist, flip in ZSLOTS])

    local = partner % (rows * NY * NZ * NC)
    marks = jnp.concatenate([local // rows, local % rows]).astype(BF).reshape(-1, 64)
    first = lax.dynamic_slice_in_dim(w_first, x * part, part, 1)
    first = jnp.pad(first, ((0, pad - share), (0, 0)))
    second = jnp.pad(w_second, ((0, pad - share), (0, part - width)))
    second = second.at[: marks.shape[0], width : width + 64].set(marks)
    near = gather_y(jnp.concatenate([first, second], axis=0))
    chosen = sum(jnp.where((y - k) % NY == x, near[k][pad:, :width], 0) for k in range(NY))
    chosen = jnp.pad(chosen, ((0, 0), (0, part - width)))
    packed = gather_zc(jnp.concatenate([n[:pad] for n in near] + [chosen], axis=0))
    packed = packed.reshape(16, NY + 1, pad, part)
    first = packed[:, :NY].reshape(16 * NY * pad, part)
    second_rel = packed[:, NY, :, :width].reshape(16 * pad, width)

    col = jnp.arange(16 * NY * pad, dtype=jnp.int32)
    slot_f = (y - col // pad % NY) % NY * (NZ * NC) + jnp.repeat(zslot, NY * pad)
    place = jnp.where(col % pad < share, slot_f * share + col % pad, -1)
    spread = (jnp.arange(depth, dtype=jnp.int32)[:, None] == place[None, :]).astype(BF)
    col = jnp.arange(16 * pad, dtype=jnp.int32)
    place = jnp.where(col % pad < share, jnp.repeat(zslot, pad) * share + col % pad, -1)
    spread_hid = (jnp.arange(part, dtype=jnp.int32)[:, None] == place[None, :]).astype(BF)

    feats = dot(jnp.concatenate(gather_x(features), axis=0), spread).astype(BF)
    second = dot(spread_hid, second_rel).astype(BF)
    pre = dot(feats, first)
    act = jnp.maximum(pre, 0.0).astype(BF)
    proj = dot(act, second).reshape(NX, rows, width)
    proj = proj[0] + sum(move_x(proj[k], -k) for k in range(1, NX))
    norm = jnp.sqrt(jnp.sum(proj * proj, axis=1) + EPSILON)
    unit = proj / norm[:, None]
    emb = unit.astype(BF)

    left = gather_zc(emb)
    right = jnp.concatenate(gather_x(jnp.concatenate(gather_y(emb), axis=0)), axis=0)
    sim = dot_nt(left, right) / TEMPER
    total = left.shape[0]
    own = jnp.arange(total, dtype=jnp.int32)
    diag = (own[:, None] == own[None, :]) & (own < rows)[:, None]
    expd = jnp.where(diag, 0.0, jnp.exp(sim - 1.0 / TEMPER))
    mate_key = jnp.concatenate([n[pad : pad + marks.shape[0], width : width + 64].reshape(2, rows) for n in near], axis=1)
    mate_key = mate_key.astype(F32)
    mate_key = mate_key[0] * rows + mate_key[1]
    mate_key = jnp.concatenate([mate_key, jnp.full((total - NY * rows,), -1.0, F32)])
    left_key = ((y * NZ * NC + zslot)[:, None] * rows + jnp.arange(rows, dtype=jnp.int32)).reshape(-1).astype(F32)
    hit = left_key[:, None] == mate_key[None, :]
    spos = jnp.sum(jnp.where(hit, sim, 0.0))

    zc_ids = jnp.arange(16, dtype=jnp.int32)
    ztable = zslot[None, :] == zc_ids[:, None]
    xy_slot = (x - zc_ids // NY) % NX * NY + (y - zc_ids % NY) % NY
    xytable = xy_slot[None, :] == zc_ids[:, None]
    row_sum = reorder(ztable, jnp.sum(expd, axis=1).reshape(16, rows))
    col_sum = reorder(xytable, jnp.sum(expd, axis=0).reshape(16, rows))
    row_sum = total_z(row_sum + swap(row_sum))
    col_sum = total_y(total_x(col_sum))
    row_sum = reorder(ztable.T, row_sum).reshape(-1)
    col_sum = reorder(xytable.T, col_sum).reshape(-1)
    lse = jnp.log(row_sum[:rows]) + 1.0 / TEMPER
    loss = jnp.sum(lse) - spos

    weight = expd * ((1.0 / row_sum)[:, None] + (1.0 / col_sum)[None, :])
    weight = jnp.where(hit, weight - 2.0, weight).astype(BF)
    grad_emb = scatter_zc(dot(weight, right)) / TEMPER
    dproj = ((grad_emb - unit * jnp.sum(unit * grad_emb, axis=1, keepdims=True)) / norm[:, None]).astype(BF)

    dproj = jnp.concatenate(gather_x(dproj), axis=0)
    dact = dot_nt(dproj, second)
    dpre = jnp.where(pre > 0.0, dact, 0.0).astype(BF)
    first_std = dot(spread, first).astype(BF)
    gfeat = dot_nt(dpre, first_std).astype(BF).reshape(NX, rows, depth)
    gfeat = sum((move_x(gfeat[k], -k) for k in range(1, NX)), gfeat[0].astype(F32)).astype(BF)
    grad_first = dot_tn(feats, dpre).reshape(16, NY * pad, part)
    grad_second = dot_tn(dot(act, spread_hid).astype(BF), dproj).reshape(16, pad, width)
    tail = jnp.full((16, pad, part - width), loss, F32)
    grads = jnp.concatenate([grad_first, jnp.concatenate([grad_second, tail], axis=2)], axis=1)
    grads = scatter_zc(grads.reshape(16 * (NY + 1) * pad, part)).reshape(NY + 1, pad, part)
    send = [jnp.concatenate([grads[k], grads[NY]], axis=0) for k in range(NY)]
    grads = send[0] + sum(move_y(send[k], -k) for k in range(1, NY))
    grads = jnp.stack(gather_x(grads))
    planes = (x - jnp.arange(NX, dtype=jnp.int32)) % NX
    count = jnp.float32(rows * NX * NY * NZ * NC)
    scale = 1.0 / jnp.sqrt(count)
    table = planes[None, :] == jnp.arange(NX, dtype=jnp.int32)[:, None]
    top = reorder(table, grads[:, :share].reshape(NX, -1)).reshape(NX, share, part) * scale
    out_first = jnp.concatenate([top[k] for k in range(NX)], axis=1)
    out_second = jnp.sum(jnp.where((planes == y)[:, None, None], grads[:, pad : pad + share, :width], 0.0), axis=0) * scale
    loss = jnp.sum(grads[:, pad, width]) / count
    return (loss, gfeat, out_first, out_second)


def solution(mesh):
    return jax.shard_map(
        on_device,
        mesh=mesh,
        in_specs=(P(("dp", "fsdp"), None), P("fsdp", None), P("fsdp", None), P(("dp", "fsdp"))),
        out_specs=(P(), P(("dp", "fsdp"), None), P("fsdp", None), P("fsdp", None)),
        check_vma=False,
    )
```

```python
import jax
import jax.numpy as jnp
from jax import lax
from jax.sharding import PartitionSpec as P

TEMPER = 0.1
EPSILON = 1e-06
NX, NY, NZ, NC = 4, 4, 8, 2
BF = jnp.bfloat16
F32 = jnp.float32

OWN = [(1, 0), (1, 1), (1, 2), (1, 3), (1, 4), (-1, 1), (-1, 2), (-1, 3)]
ZSLOTS = [(g, s, 0) for g, s in OWN] + [(-g, s, 1) for g, s in OWN]


def fsdp_perm(place):
    pairs = []
    for y in range(NY):
        for z in range(NZ):
            for c in range(NC):
                y2, z2, c2 = place(y, z, c)
                pairs.append(((y * NZ + z) * NC + c, ((y2 % NY) * NZ + z2 % NZ) * NC + c2))
    return pairs


PERM_SWAP = fsdp_perm(lambda y, z, c: (y, z, 1 - c))
PERM_RING = fsdp_perm(lambda y, z, c: (y, z + 1 - 2 * c, c))
PERM_BACK = fsdp_perm(lambda y, z, c: (y, z - 1 + 2 * c, c))


def swap(v):
    return lax.ppermute(v, "fsdp", PERM_SWAP)


def ring(v):
    return lax.ppermute(v, "fsdp", PERM_RING)


def back(v):
    return lax.ppermute(v, "fsdp", PERM_BACK)


def move_y(v, by):
    return lax.ppermute(v, "fsdp", fsdp_perm(lambda y, z, c: (y + by, z, c)))


def move_z(v, by):
    return lax.ppermute(v, "fsdp", fsdp_perm(lambda y, z, c: (y, z + by, c)))


def move_x(v, by):
    return lax.ppermute(v, "dp", [(i, (i + by) % NX) for i in range(NX)])


def gather_y(v):
    return [v] + [move_y(v, k) for k in range(1, NY)]


def gather_x(v):
    return [v] + [move_x(v, k) for k in range(1, NX)]


def gather_z(v):
    mine, other = [v], [v]
    for step in range(1, 5):
        mine.append(ring(mine[-1]))
        if step < 4:
            other.append(back(other[-1]))
    return jnp.concatenate(mine + other[1:], axis=0)


def gather_zc_split(v):
    m = v.shape[0]
    block = jnp.concatenate([v, swap(v)], axis=0)
    one = ring(block)
    two = ring(one)
    three = ring(two)
    four = ring(three[:m])
    got = swap(jnp.concatenate([one, two, three, four], axis=0))
    own = [block[:m], one[:m], two[:m], three[:m], four] + [got[k * m : (k + 1) * m] for k in (1, 3, 5)]
    other = [block[m:], got[:m], got[2 * m : 3 * m], got[4 * m : 5 * m], got[6 * m :], one[m:], two[m:], three[m:]]
    return jnp.concatenate(own + other, axis=0), one


def scatter_z(v):
    slot = [v[k * (v.shape[0] // 8) : (k + 1) * (v.shape[0] // 8)] for k in range(8)]
    mine, other = slot[4], slot[7]
    for k in (3, 2, 1):
        mine = back(mine) + slot[k]
    for k in (6, 5):
        other = ring(other) + slot[k]
    return slot[0] + back(mine) + ring(other)


def total_z(v):
    low, high = move_z(v, 1), move_z(v, -1)
    part = v + low
    return part + high + move_z(part + high, 3) + move_z(part, -3)


def total_x(v):
    return sum(gather_x(v))


def total_y(v):
    return sum(gather_y(v))


def dot(a, b):
    return jnp.dot(a, b, preferred_element_type=F32)


def dot_nt(a, b):
    return lax.dot_general(a, b, (((1,), (1,)), ((), ())), preferred_element_type=F32)


def dot_tn(a, b):
    return lax.dot_general(a, b, (((0,), (0,)), ((), ())), preferred_element_type=F32)


def reorder(table, v):
    return jnp.sum(jnp.where(table[:, :, None], v[None], 0.0), axis=1)


def on_device(features, w_first, w_second, partner):
    rows, depth = features.shape
    hidden, width = w_second.shape[0] * NY * NZ * NC, w_second.shape[1]
    share = depth // (NY * NZ * NC)
    pad = -(-share // 8) * 8
    part = hidden // NX
    x = lax.axis_index("dp")
    f = lax.axis_index("fsdp")
    y, z, c = f // (NZ * NC), f // NC % NZ, f % NC
    step = 1 - 2 * c
    zslot = jnp.stack([(z - sign * dist * step) % NZ * NC + (c ^ flip) for sign, dist, flip in ZSLOTS])

    local = partner % (rows * NY * NZ * NC)
    marks = jnp.concatenate([local // rows, local % rows]).astype(BF)[None, :]
    marks = jnp.pad(marks, ((0, 7), (0, part - 2 * rows)))
    first = sum(jnp.where(x == k, w_first[:, k * part : (k + 1) * part], 0) for k in range(NX))
    first = jnp.pad(first, ((0, pad - share), (0, 0)))
    second = jnp.pad(w_second, ((0, pad - share), (0, part - width)))
    near = gather_y(jnp.concatenate([first, second, marks], axis=0))
    near, features_x = lax.optimization_barrier((near, features))
    chosen = sum(jnp.where((y - k) % NY == x, near[k][pad : 2 * pad], 0) for k in range(NY))
    block = (NY + 1) * pad
    packed = gather_z(jnp.concatenate([n[:pad] for n in near] + [chosen], axis=0))
    packed = (packed, swap(packed))
    mate_key = jnp.concatenate([n[2 * pad, :rows].astype(F32) * rows + n[2 * pad, rows : 2 * rows] for n in near])

    def places(slots):
        col = jnp.arange(8 * block, dtype=jnp.int32)
        line, kind = col % pad, col % block // pad
        slot = jnp.repeat(slots, block)
        col_first = ((y - kind) % NY * (NZ * NC) + slot) * share + line
        col_second = slot * share + line
        col_first = jnp.where((kind < NY) & (line < share), col_first, -1)
        col_second = jnp.where((kind == NY) & (line < share), col_second, -1)
        spread = (jnp.arange(depth, dtype=jnp.int32)[:, None] == col_first[None, :]).astype(BF)
        spread_hid = (jnp.arange(part, dtype=jnp.int32)[:, None] == col_second[None, :]).astype(BF)
        return spread, spread_hid, (kind == NY) & (line == 0)

    place = (places(zslot[:8]), places(zslot[8:]))

    feats = jnp.concatenate(gather_x(features_x), axis=0)
    feats = [dot(feats, spread).astype(BF) for spread, _, _ in place]
    second = sum(dot(spread_hid, w) for (_, spread_hid, _), w in zip(place, packed))[:, :width].astype(BF)
    pre = dot(feats[0], packed[0]) + dot(feats[1], packed[1])
    act = jnp.maximum(pre, 0.0).astype(BF)
    proj = dot(act, second).reshape(NX, rows, width)
    proj = proj[0] + sum(move_x(proj[k], -k) for k in range(1, NX))
    norm = jnp.sqrt(jnp.sum(proj * proj, axis=1) + EPSILON)
    unit = proj / norm[:, None]
    emb = unit.astype(BF)

    left, one = gather_zc_split(emb)
    emb_y, one = lax.optimization_barrier((emb, one))
    right = jnp.concatenate(gather_x(jnp.concatenate(gather_y(emb_y), axis=0)), axis=0)
    sim = dot_nt(left, right) / TEMPER
    total = left.shape[0]
    own = jnp.arange(total, dtype=jnp.int32)
    diag = (own[:, None] == own[None, :]) & (own < rows)[:, None]
    expd = jnp.where(diag, 0.0, jnp.exp(sim - 1.0 / TEMPER))
    mate_key = jnp.concatenate([mate_key, jnp.full((total - NY * rows,), -1.0, F32)])
    left_key = ((y * NZ * NC + zslot)[:, None] * rows + jnp.arange(rows, dtype=jnp.int32)).reshape(-1).astype(F32)
    hit = left_key[:, None] == mate_key[None, :]
    spos = jnp.sum(jnp.where(hit, sim, 0.0))

    zc_ids = jnp.arange(16, dtype=jnp.int32)
    ztable = zslot[None, :] == zc_ids[:, None]
    xy_slot = (x - zc_ids // NY) % NX * NY + (y - zc_ids % NY) % NY
    xytable = xy_slot[None, :] == zc_ids[:, None]
    row_sum = reorder(ztable, jnp.sum(expd, axis=1).reshape(16, rows))
    col_sum = reorder(xytable, jnp.sum(expd, axis=0).reshape(16, rows))
    row_sum = total_z(row_sum + swap(row_sum))
    col_sum = total_y(total_x(col_sum))
    row_sum = reorder(ztable.T, row_sum).reshape(-1)
    col_sum = reorder(xytable.T, col_sum).reshape(-1)
    lse = jnp.log(row_sum[:rows]) + 1.0 / TEMPER
    loss = jnp.sum(lse) - spos

    weight = expd * ((1.0 / row_sum)[:, None] + (1.0 / col_sum)[None, :])
    weight = jnp.where(hit, weight - 2.0, weight).astype(BF)
    grad_emb = dot(weight, right)
    grad_emb = grad_emb[: total // 2] + swap(grad_emb[total // 2 :])
    grad_emb = scatter_z(grad_emb) / TEMPER
    dproj = ((grad_emb - unit * jnp.sum(unit * grad_emb, axis=1, keepdims=True)) / norm[:, None]).astype(BF)

    dproj = jnp.concatenate(gather_x(dproj), axis=0)
    dact = dot_nt(dproj, second)
    dpre = jnp.where(pre > 0.0, dact, 0.0).astype(BF)
    wide = jnp.pad(dproj, ((0, 0), (0, part - width)))
    lane = jnp.arange(part, dtype=jnp.int32) == width
    grads = []
    for feat, (_, spread_hid, mark) in zip(feats, place):
        grad = dot_tn(feat, dpre) + dot_tn(dot(act, spread_hid).astype(BF), wide)
        grads.append(grad + jnp.where(mark[:, None] & lane[None, :], loss, 0.0))
    grads = scatter_z(grads[0] + swap(grads[1])).reshape(NY + 1, pad, part)
    first_std = sum(dot(spread, w) for (spread, _, _), w in zip(place, packed)).astype(BF)
    gfeat = dot_nt(dpre, first_std).astype(BF).reshape(NX, rows, depth)
    gfeat = sum((move_x(gfeat[k], -k) for k in range(1, NX)), gfeat[0].astype(F32)).astype(BF)
    send = [jnp.concatenate([grads[k], grads[NY]], axis=0) for k in range(NY)]
    grads = send[0] + sum(move_y(send[k], -k) for k in range(1, NY))
    grads = jnp.stack(gather_x(grads))
    planes = (x - jnp.arange(NX, dtype=jnp.int32)) % NX
    count = jnp.float32(rows * NX * NY * NZ * NC)
    scale = 1.0 / jnp.sqrt(count)
    table = planes[None, :] == jnp.arange(NX, dtype=jnp.int32)[:, None]
    top = reorder(table, grads[:, :share].reshape(NX, -1)).reshape(NX, share, part) * scale
    out_first = jnp.concatenate([top[k] for k in range(NX)], axis=1)
    out_second = jnp.sum(jnp.where((planes == y)[:, None, None], grads[:, pad : pad + share, :width], 0.0), axis=0) * scale
    loss = jnp.sum(grads[:, pad, width]) / count
    return (loss, gfeat, out_first, out_second)


def solution(mesh):
    return jax.shard_map(
        on_device,
        mesh=mesh,
        in_specs=(P(("dp", "fsdp"), None), P("fsdp", None), P("fsdp", None), P(("dp", "fsdp"))),
        out_specs=(P(), P(("dp", "fsdp"), None), P("fsdp", None), P("fsdp", None)),
        check_vma=False,
    )
```

```python
import jax
import jax.numpy as jnp
from jax import lax
from jax.sharding import PartitionSpec as P

TEMPER = 0.1
EPSILON = 1e-06
NX, NY, NZ, NC = 4, 4, 8, 2
BF = jnp.bfloat16
F32 = jnp.float32


def fsdp_perm(place):
    pairs = []
    for y in range(NY):
        for z in range(NZ):
            for c in range(NC):
                y2, z2, c2 = place(y, z, c)
                pairs.append(((y * NZ + z) * NC + c, (y2 * NZ + z2 % NZ) * NC + c2))
    return pairs


def swap(v):
    return lax.ppermute(v, "fsdp", fsdp_perm(lambda y, z, c: (y, z, 1 - c)))


def move_z(v, by):
    return lax.ppermute(v, "fsdp", fsdp_perm(lambda y, z, c: (y, z + by, c)))


def flip_y(v, k):
    return lax.ppermute(v, "fsdp", fsdp_perm(lambda y, z, c: (y ^ k, z, c)))


def flip_x(v, j):
    return lax.ppermute(v, "dp", [(i, i ^ j) for i in range(NX)])


def tie(*values):
    return lax.optimization_barrier(values)


def gather_y(v):
    return [v] + [flip_y(v, k) for k in range(1, NY)]


def gather_x(v):
    return [v] + [flip_x(v, j) for j in range(1, NX)]


def gather_z(v, beside=()):
    up, down, done = [v], [v], []
    for step in range(1, 5):
        if step <= len(beside):
            extra, now_up, now_down = tie(beside[step - 1](), up[-1], down[-1])
            done.append(extra)
        else:
            now_up, now_down = up[-1], down[-1]
        up.append(move_z(now_up, 1))
        if step < 4:
            down.append(move_z(now_down, -1))
    return [v] + down[1:] + up[:0:-1], done


def scatter_x(v):
    return v[0] + sum(flip_x(v[j], j) for j in range(1, NX))


def scatter_z(slot):
    up, down = slot[4], slot[5]
    for dz in (3, 2, 1):
        up = move_z(up, 1) + slot[dz]
    for dz in (6, 7):
        down = move_z(down, -1) + slot[dz]
    return slot[0] + move_z(up, 1) + move_z(down, -1)


def dot(a, b):
    return jnp.dot(a, b, preferred_element_type=F32)


def dot_nt(a, b):
    return lax.dot_general(a, b, (((1,), (1,)), ((), ())), preferred_element_type=F32)


def on_device(features, w_first, w_second, partner):
    rows, depth = features.shape
    hidden, width = w_second.shape[0] * NY * NZ * NC, w_second.shape[1]
    share = depth // (NY * NZ * NC)
    pad = -(-share // 8) * 8
    part = hidden // NX
    x = lax.axis_index("dp")
    f = lax.axis_index("fsdp")
    y, z, c = f // (NZ * NC), f // NC % NZ, f % NC

    first = sum(jnp.where(x == k, w_first[:, k * part : (k + 1) * part], 0) for k in range(NX))
    first = jnp.pad(first, ((0, pad - share), (0, 0)))
    second = jnp.pad(w_second, ((0, pad - share), (0, part - width)))
    near = gather_y(jnp.concatenate([first, second], axis=0))
    block = (NY + 1) * pad

    def places(flip):
        col = jnp.arange(NZ * block, dtype=jnp.int32)
        line, kind = col % pad, col % block // pad
        slot = (z + col // block) % NZ * NC + (c ^ flip)
        col_first = ((y ^ kind) * (NZ * NC) + slot) * share + line
        col_second = slot * share + line
        col_first = jnp.where((kind < NY) & (line < share), col_first, -1)
        col_second = jnp.where((kind == NY) & (line < share), col_second, -1)
        spread = (jnp.arange(depth, dtype=jnp.int32)[:, None] == col_first[None, :]).astype(BF)
        spread_hid = (jnp.arange(part, dtype=jnp.int32)[:, None] == col_second[None, :]).astype(BF)
        return spread, spread_hid, (kind == NY) & (line == 0)

    (spread_a, hid_a, mark_a), (spread_b, hid_b, mark_b) = places(0), places(1)
    local = partner % (rows * NY * NZ * NC)
    mate_other = swap(local.astype(F32)[None, :])
    near, spread_a, spread_b, hid_a, hid_b, mate_other = tie(near, spread_a, spread_b, hid_a, hid_b, mate_other)
    chosen = sum(jnp.where((y ^ k) == x, near[k][pad:], 0) for k in range(NY))

    feats, moved = [], [features]

    def spread_rows(value):
        return dot(value, spread_a).astype(BF), dot(value, spread_b).astype(BF)

    def ride(v, last, j):
        value, last = tie(v, last)
        moved.append(flip_x(value, j))
        return last

    start = jnp.concatenate([n[:pad] for n in near] + [chosen], axis=0)
    up, down = [start], [start]
    for step in range(1, 5):
        now_up, now_down = up[-1], down[-1]
        if step < 4:
            now_up = ride(features, now_up, step)
        if step > 2:
            feat, now_up, now_down = tie(spread_rows(moved[step - 3]), now_up, now_down)
            feats.append(feat)
        up.append(move_z(now_up, 1))
        if step < 4:
            down.append(move_z(now_down, -1))
    half_a = jnp.concatenate([start] + down[1:] + up[:0:-1], axis=0)
    feat, half_a = tie(spread_rows(moved[2]), half_a)
    feats.append(feat)
    half_b = swap(half_a)
    feats.append(spread_rows(moved[3]))
    feat_a, feat_b = (jnp.concatenate([v[h] for v in feats], axis=0) for h in (0, 1))

    second = (dot(hid_a, half_a) + dot(hid_b, half_b))[:, :width].astype(BF)
    pre = dot(feat_a, half_a) + dot(feat_b, half_b)
    act = jnp.maximum(pre, 0.0).astype(BF)
    proj = scatter_x(dot(act, second).reshape(NX, rows, width))
    norm = jnp.sqrt(jnp.sum(proj * proj, axis=1) + EPSILON)
    unit = proj / norm[:, None]
    emb = unit.astype(BF)

    def for_grad(feat, hid):
        return jnp.concatenate([feat, dot(act, hid).astype(BF)], axis=0).T

    right = jnp.concatenate(gather_y(emb), axis=0)
    right, emb_x = tie(right, emb)
    right, early = gather_z(
        right,
        (
            lambda: jnp.zeros((), F32),
            lambda: (dot(spread_a, half_a) + dot(spread_b, half_b)).astype(BF),
            lambda: for_grad(feat_a, hid_a),
            lambda: for_grad(feat_b, hid_b),
        ),
    )
    _, first_std, for_grad_a, for_grad_b = early
    right = jnp.concatenate(right, axis=0)
    left = jnp.concatenate(gather_x(emb_x), axis=0)
    left = jnp.concatenate([left, swap(left)], axis=0)
    sim = dot_nt(left, right) / TEMPER
    n_left, n_right = sim.shape
    at_left, at_right = jnp.arange(n_left, dtype=jnp.int32), jnp.arange(n_right, dtype=jnp.int32)
    diag = (at_left[:, None] == at_right[None, :]) & (at_left < rows)[:, None]
    expd = jnp.where(diag, 0.0, jnp.exp(sim - 1.0 / TEMPER))
    slot = at_right // rows
    key = (((y ^ slot % NY) * NZ + (z + slot // NY) % NZ) * NC + c) * rows + at_right % rows
    gap = jnp.full(((NX - 1) * rows,), -1.0, F32)
    mate_key = jnp.concatenate([local.astype(F32), gap, mate_other[0], gap])
    hit = mate_key[:, None] == key.astype(F32)[None, :]
    spos = jnp.sum(jnp.where(hit, sim, 0.0))

    row_sum = jnp.sum(expd, axis=1).reshape(NC, NX, rows)
    col_sum = jnp.sum(expd, axis=0).reshape(NZ, NY, rows)
    for k in (1, 2):
        got_y, got_x = flip_y(col_sum, k), flip_x(row_sum, k)
        col_sum = col_sum + jnp.stack([got_y[:, i ^ k] for i in range(NY)], axis=1)
        row_sum = row_sum + jnp.stack([got_x[:, i ^ k] for i in range(NX)], axis=1)
    row_sum = row_sum + swap(row_sum)[::-1]
    two = col_sum + jnp.roll(move_z(col_sum, 1), -1, axis=0)
    three = two + jnp.roll(move_z(col_sum, -1), 1, axis=0)
    col_sum = three + jnp.roll(move_z(three, 3), -3, axis=0) + jnp.roll(move_z(two, -3), 3, axis=0)
    lse = jnp.log(row_sum[0, 0]) + 1.0 / TEMPER
    loss = jnp.sum(lse) - spos

    weight = expd * ((1.0 / row_sum).reshape(-1)[:, None] + (1.0 / col_sum).reshape(-1)[None, :])
    weight = jnp.where(hit, weight - 2.0, weight).astype(BF)
    grad_emb = dot(weight, right)
    grad_emb = grad_emb[: n_left // 2] + swap(grad_emb[n_left // 2 :])
    grad_emb = scatter_x(grad_emb.reshape(NX, rows, width)) / TEMPER
    dproj = ((grad_emb - unit * jnp.sum(unit * grad_emb, axis=1, keepdims=True)) / norm[:, None]).astype(BF)

    dproj = jnp.concatenate(gather_x(dproj), axis=0)
    dact = dot_nt(dproj, second)
    dpre = jnp.where(pre > 0.0, dact, 0.0).astype(BF)
    both = jnp.concatenate([dpre, jnp.pad(dproj, ((0, 0), (0, part - width)))], axis=0)
    lane = jnp.arange(part, dtype=jnp.int32) == width
    grad_b = dot(for_grad_b, both) + jnp.where(mark_b[:, None] & lane[None, :], loss, 0.0)
    got = swap(grad_b)
    grad_a = dot(for_grad_a, both) + jnp.where(mark_a[:, None] & lane[None, :], loss, 0.0)
    grads = (grad_a + got).reshape(NZ, block, part)
    grads = scatter_z([grads[dz] for dz in range(NZ)]).reshape(NY + 1, pad, part)
    gfeat = dot_nt(dpre, first_std).astype(BF).reshape(NX, rows, depth)
    gfeat = sum((flip_x(gfeat[j], j) for j in range(1, NX)), gfeat[0].astype(F32)).astype(BF)
    send = [jnp.concatenate([grads[k], grads[NY]], axis=0) for k in range(NY)]
    grads = jnp.stack(gather_x(send[0] + sum(flip_y(send[k], k) for k in range(1, NY))))
    count = jnp.float32(rows * NX * NY * NZ * NC)
    scale = 1.0 / jnp.sqrt(count)
    out_first = []
    for plane in range(NX):
        out_first.append(sum(jnp.where((x ^ j) == plane, grads[j, :share], 0.0) for j in range(NX)) * scale)
    out_first = jnp.concatenate(out_first, axis=1)
    out_second = sum(jnp.where((x ^ j) == y, grads[j, pad : pad + share, :width], 0.0) for j in range(NX)) * scale
    loss = jnp.sum(grads[:, pad, width]) / count
    return (loss, gfeat, out_first, out_second)


def solution(mesh):
    return jax.shard_map(
        on_device,
        mesh=mesh,
        in_specs=(P(("dp", "fsdp"), None), P("fsdp", None), P("fsdp", None), P(("dp", "fsdp"))),
        out_specs=(P(), P(("dp", "fsdp"), None), P("fsdp", None), P("fsdp", None)),
        check_vma=False,
    )
```

```python
import jax
import jax.numpy as jnp
from jax import lax
from jax.sharding import PartitionSpec as P

TEMPER = 0.1
EPSILON = 1e-06
NX, NY, NZ, NC = 4, 4, 8, 2
BF = jnp.bfloat16
F32 = jnp.float32


def fsdp_perm(place):
    pairs = []
    for y in range(NY):
        for z in range(NZ):
            for c in range(NC):
                y2, z2, c2 = place(y, z, c)
                pairs.append(((y * NZ + z) * NC + c, (y2 * NZ + z2 % NZ) * NC + c2))
    return pairs


def swap(v):
    return lax.ppermute(v, "fsdp", fsdp_perm(lambda y, z, c: (y, z, 1 - c)))


def move_z(v, by):
    return lax.ppermute(v, "fsdp", fsdp_perm(lambda y, z, c: (y, z + by, c)))


def flip_y(v, k):
    return lax.ppermute(v, "fsdp", fsdp_perm(lambda y, z, c: (y ^ k, z, c)))


def flip_x(v, j):
    return lax.ppermute(v, "dp", [(i, i ^ j) for i in range(NX)])


def tie(*values):
    return lax.optimization_barrier(values)


def gather_y(v):
    return [v] + [flip_y(v, k) for k in range(1, NY)]


def gather_x(v):
    return [v] + [flip_x(v, j) for j in range(1, NX)]


def gather_z(v, beside=()):
    up, down, made = [v], [v], []
    for step in range(1, 5):
        now_up, now_down = up[-1], down[-1]
        if step <= len(beside) and beside[step - 1] is not None:
            extra, now_up, now_down = tie(beside[step - 1](now_up), now_up, now_down)
            made.append(extra)
        if step < 4:
            up.append(move_z(now_up, 1))
            down.append(move_z(now_down, -1))
    half = v.shape[0] // 2
    far = [move_z(now_up[:half], 1), move_z(now_down[half:], -1)]
    return [v] + down[1:] + far + up[:0:-1], made


def scatter_x(v):
    return v[0] + sum(flip_x(v[j], j) for j in range(1, NX))


def scatter_z(slot, beside):
    def move(v, by):
        return move_z(v.astype(BF), by).astype(F32)

    up, down = slot[4], slot[5]
    for dz in (3, 2, 1):
        up = move(up, 1) + slot[dz]
    for dz in (6, 7):
        down = move(down, -1) + slot[dz]
    beside, up = tie(beside, up)
    return slot[0] + move(up, 1) + move(down, -1), beside


def dot(a, b):
    return jnp.dot(a, b, preferred_element_type=F32)


def dot_nt(a, b):
    return lax.dot_general(a, b, (((1,), (1,)), ((), ())), preferred_element_type=F32)


def on_device(features, w_first, w_second, partner):
    rows, depth = features.shape
    hidden, width = w_second.shape[0] * NY * NZ * NC, w_second.shape[1]
    share = depth // (NY * NZ * NC)
    pad = -(-share // 8) * 8
    part = hidden // NX
    x = lax.axis_index("dp")
    f = lax.axis_index("fsdp")
    y, z, c = f // (NZ * NC), f // NC % NZ, f % NC

    first = sum(jnp.where(x == k, w_first[:, k * part : (k + 1) * part], 0) for k in range(NX))
    first = jnp.pad(first, ((0, pad - share), (0, 0)))
    second = jnp.pad(w_second, ((0, pad - share), (0, part - width)))
    near = gather_y(jnp.concatenate([first, second], axis=0))
    block = (NY + 1) * pad

    def places(flip):
        col = jnp.arange(NZ * block, dtype=jnp.int32)
        line, kind = col % pad, col % block // pad
        slot = (z + col // block) % NZ * NC + (c ^ flip)
        row = jnp.where(kind < NY, ((y ^ kind) * (NZ * NC) + slot) * share, depth + slot * share) + line
        row = jnp.where(line < share, row, -1)
        spread = (jnp.arange(depth + part, dtype=jnp.int32)[:, None] == row[None, :]).astype(BF)
        return spread, (kind == NY) & (line == 0)

    local = partner % (rows * NY * NZ * NC)
    chosen = sum(jnp.where((y ^ k) == x, near[k][pad:], 0) for k in range(NY))
    (spread_a, mark_a), (spread_b, mark_b) = places(0), places(1)

    start = jnp.concatenate([n[:pad] for n in near] + [chosen], axis=0)
    up, down, feats = [start], [start], [features]
    for step in range(1, 5):
        now_up, now_down = up[-1], down[-1]
        if step > 1:
            value, now_up, now_down = tie(features, now_up, now_down)
        if step == 3:
            spread_a, now_up, now_down = tie(spread_a, now_up, now_down)
        if step == 4:
            spread_b, now_up = tie(spread_b, now_up)
        up.append(move_z(now_up, 1))
        if step < 4:
            down.append(move_z(now_down, -1))
        if step > 1:
            feats.append(flip_x(value, step - 1))
    half_a = jnp.concatenate([start] + down[1:] + up[:0:-1], axis=0)
    half_b = swap(half_a)
    mate_other = swap(local.astype(F32)[None, :])
    feats = jnp.concatenate(feats, axis=0)

    whole, half_b = tie(dot(spread_a, half_a), half_b)
    whole = (whole + dot(spread_b, half_b)).astype(BF)
    first, second = whole[:depth], whole[depth:, :width]
    pre = dot(feats, first)
    act = jnp.maximum(pre, 0.0).astype(BF)
    proj = scatter_x(dot(act, second).reshape(NX, rows, width))
    norm = jnp.sqrt(jnp.sum(proj * proj, axis=1) + EPSILON)
    unit = proj / norm[:, None]
    emb = unit.astype(BF)

    def turned(spread, value):
        return lax.dot_general(spread, value, (((0,), (1,)), ((), ())), preferred_element_type=F32).astype(BF)

    right = jnp.concatenate(gather_y(emb), axis=0)
    right, emb_x, feats, act = tie(right, emb, feats, act)
    right, made = gather_z(
        right,
        (
            None,
            lambda after: turned(spread_a[:depth], feats),
            lambda after: turned(spread_b[:depth], feats),
            lambda after: (turned(spread_a[depth:], act), turned(spread_b[depth:], act)),
        ),
    )
    feat_a, feat_b, (act_a, act_b) = made
    right = jnp.concatenate(right, axis=0)
    left = jnp.concatenate(gather_x(emb_x), axis=0)
    left = jnp.concatenate([left, swap(left)], axis=0)
    sim = dot_nt(left, right) / TEMPER
    n_left, n_right = sim.shape
    at_left, at_right = jnp.arange(n_left, dtype=jnp.int32), jnp.arange(n_right, dtype=jnp.int32)
    diag = (at_left[:, None] == at_right[None, :]) & (at_left < rows)[:, None]
    expd = jnp.where(diag, 0.0, jnp.exp(sim - 1.0 / TEMPER))
    slot = at_right // rows
    key = (((y ^ slot % NY) * NZ + (z + slot // NY) % NZ) * NC + c) * rows + at_right % rows
    gap = jnp.full(((NX - 1) * rows,), -1.0, F32)
    mate_key = jnp.concatenate([local.astype(F32), gap, mate_other[0], gap])
    hit = mate_key[:, None] == key.astype(F32)[None, :]
    spos = jnp.sum(jnp.where(hit, sim, 0.0))

    row_sum = jnp.sum(expd, axis=1).reshape(NC, NX, rows)
    col_sum = jnp.sum(expd, axis=0).reshape(NZ, NY, rows)
    got_x = flip_x(row_sum, 1)
    got_y = [flip_y(col_sum, k) for k in range(1, NY)]
    row_sum = row_sum + jnp.stack([got_x[:, i ^ 1] for i in range(NX)], axis=1)
    col_sum = col_sum + sum(jnp.stack([got_y[k - 1][:, i ^ k] for i in range(NY)], axis=1) for k in range(1, NY))
    got_x = flip_x(row_sum, 2)
    row_sum = row_sum + jnp.stack([got_x[:, i ^ 2] for i in range(NX)], axis=1)
    two = col_sum + jnp.roll(move_z(col_sum, 1), -1, axis=0)
    three = two + jnp.roll(move_z(col_sum, -1), 1, axis=0)
    row_sum = row_sum + swap(row_sum)[::-1]
    col_sum = three + jnp.roll(move_z(three, 3), -3, axis=0) + jnp.roll(move_z(two, -3), 3, axis=0)
    lse = jnp.log(row_sum[0, 0]) + 1.0 / TEMPER
    loss = jnp.sum(lse) - spos

    weight = expd * ((1.0 / row_sum).reshape(-1)[:, None] + (1.0 / col_sum).reshape(-1)[None, :])
    weight = jnp.where(hit, weight - 2.0, weight).astype(BF)
    grad_emb = dot(weight, right)
    grad_emb = grad_emb[: n_left // 2] + swap(grad_emb[n_left // 2 :])
    grad_emb = scatter_x(grad_emb.reshape(NX, rows, width)) / TEMPER
    dproj = ((grad_emb - unit * jnp.sum(unit * grad_emb, axis=1, keepdims=True)) / norm[:, None]).astype(BF)

    dproj = jnp.concatenate(gather_x(dproj), axis=0)
    dact = dot_nt(dproj, second)
    dpre = jnp.where(pre > 0.0, dact, 0.0).astype(BF)
    wide = jnp.pad(dproj, ((0, 0), (0, part - width)))
    lane = jnp.arange(part, dtype=jnp.int32) == width

    def grads_of(feat, acts, mark):
        return dot(feat, dpre) + dot(acts, wide) + jnp.where(mark[:, None] & lane[None, :], loss, 0.0)

    got = swap(grads_of(feat_b, act_b, mark_b).astype(BF))
    gfeat = dot_nt(dpre, first).astype(BF).reshape(NX, rows, depth)
    grads = grads_of(feat_a, act_a, mark_a)
    gfeat, grads = tie(gfeat, grads)
    grads = (grads + got.astype(F32)).reshape(NZ, block, part)
    moved = [flip_x(gfeat[j], j) for j in range(1, NX)]
    grads, moved = scatter_z([grads[dz] for dz in range(NZ)], moved)
    grads = grads.reshape(NY + 1, pad, part)
    gfeat = sum(moved, gfeat[0].astype(F32)).astype(BF)
    send = [jnp.concatenate([grads[k], grads[NY]], axis=0) for k in range(NY)]
    grads = jnp.stack(gather_x(send[0] + sum(flip_y(send[k], k) for k in range(1, NY))))
    count = jnp.float32(rows * NX * NY * NZ * NC)
    scale = 1.0 / jnp.sqrt(count)
    out_first = []
    for plane in range(NX):
        out_first.append(sum(jnp.where((x ^ j) == plane, grads[j, :share], 0.0) for j in range(NX)) * scale)
    out_first = jnp.concatenate(out_first, axis=1)
    out_second = sum(jnp.where((x ^ j) == y, grads[j, pad : pad + share, :width], 0.0) for j in range(NX)) * scale
    loss = jnp.sum(grads[:, pad, width]) / count
    return (loss, gfeat, out_first, out_second)


def solution(mesh):
    return jax.shard_map(
        on_device,
        mesh=mesh,
        in_specs=(P(("dp", "fsdp"), None), P("fsdp", None), P("fsdp", None), P(("dp", "fsdp"))),
        out_specs=(P(), P(("dp", "fsdp"), None), P("fsdp", None), P("fsdp", None)),
        check_vma=False,
    )
```

```python
import jax
import jax.numpy as jnp
from jax import lax
from jax.sharding import Mesh, PartitionSpec as P

TEMPER = 0.1
EPSILON = 1e-06
NX, NY, NZ, NC = 4, 4, 8, 2
BF = jnp.bfloat16
F32 = jnp.float32


def swap(v):
    return lax.ppermute(v, "c", [(0, 1), (1, 0)])


def flip_x(v, j):
    return lax.ppermute(v, "x", [(i, i ^ j) for i in range(NX)])


def tie(*values):
    return lax.optimization_barrier(values)


def trade(v, axes):
    return lax.all_to_all(v, axes, 0, 0, tiled=True)


def every(v, axes, size):
    return trade(jnp.broadcast_to(v[None], (size,) + v.shape), axes)


def gather_x(v):
    return [v] + [flip_x(v, j) for j in range(1, NX)]


def dot(a, b):
    return jnp.dot(a, b, preferred_element_type=F32)


def dot_nt(a, b):
    return lax.dot_general(a, b, (((1,), (1,)), ((), ())), preferred_element_type=F32)


def on_device(features, w_first, w_second, partner):
    rows, depth = features.shape
    hidden, width = w_second.shape[0] * NY * NZ * NC, w_second.shape[1]
    share = depth // (NY * NZ * NC)
    pad = -(-share // 8) * 8
    part = hidden // NX
    block = (NY + 1) * pad
    x, y, z, c = (lax.axis_index(name) for name in "xyzc")

    first = sum(jnp.where(x == k, w_first[:, k * part : (k + 1) * part], 0) for k in range(NX))
    first = jnp.pad(first, ((0, pad - share), (0, 0)))
    second = jnp.pad(w_second, ((0, pad - share), (0, part - width)))
    local = partner % (rows * NY * NZ * NC)
    marks = jnp.concatenate([local // rows, local % rows]).astype(BF)[None, :]
    marks = jnp.pad(marks, ((0, 7), (0, part - 2 * rows)))
    near = every(jnp.concatenate([first, second, marks], axis=0), "y", NY)
    mates = near[:, 2 * pad, :rows].astype(F32) * rows + near[:, 2 * pad, rows : 2 * rows].astype(F32)
    chosen = lax.dynamic_index_in_dim(near, x, 0, False)[pad : 2 * pad]

    features, near = tie(features, near)
    moved = [features] + [flip_x(features, j) for j in range(1, NX)]
    half_a = every(jnp.concatenate([near[k, :pad] for k in range(NY)] + [chosen], axis=0), "z", NZ)
    half_a = half_a.reshape(NZ * block, part)
    half_b = swap(half_a)

    def places(flip):
        col = jnp.arange(NZ * block, dtype=jnp.int32)
        line, kind = col % pad, col % block // pad
        slot = col // block * NC + (c ^ flip)
        row = jnp.where(kind < NY, (kind * (NZ * NC) + slot) * share, depth + slot * share) + line
        row = jnp.where(line < share, row, -1)
        spread = (jnp.arange(depth + part, dtype=jnp.int32)[:, None] == row[None, :]).astype(BF)
        return spread, (kind == NY) & (line == 0)

    (spread_a, mark_a), (spread_b, mark_b) = places(0), places(1)
    feats = jnp.concatenate(moved, axis=0)

    whole, half_b = tie(dot(spread_a, half_a), half_b)
    whole = (whole + dot(spread_b, half_b)).astype(BF)
    first, second = whole[:depth], whole[depth:, :width]
    pre = dot(feats, first)
    act = jnp.maximum(pre, 0.0).astype(BF)
    proj, feats, act = tie(dot(act, second).reshape(NX, rows, width), feats, act)
    moved = [flip_x(proj[j], j) for j in range(1, NX)]

    def turned(spread, value):
        return lax.dot_general(spread, value, (((0,), (1,)), ((), ())), preferred_element_type=F32).astype(BF)

    feat_a, feat_b = turned(spread_a[:depth], feats), turned(spread_b[:depth], feats)
    act_a, act_b = turned(spread_a[depth:], act), turned(spread_b[depth:], act)
    moved, feat_a, feat_b, act_a, act_b = tie(moved, feat_a, feat_b, act_a, act_b)
    proj = sum(moved, proj[0])
    norm = jnp.sqrt(jnp.sum(proj * proj, axis=1) + EPSILON)
    unit = proj / norm[:, None]
    emb = unit.astype(BF)

    right = every(emb, "z", NZ).reshape(NZ * rows, width)
    right = jnp.concatenate([right, swap(right)], axis=0)
    left = every(emb, ("x", "y"), NX * NY).reshape(NX * NY * rows, width)
    sim = dot_nt(left, right) / TEMPER
    n_left, n_right = sim.shape
    at_left, at_right = jnp.arange(n_left, dtype=jnp.int32), jnp.arange(n_right, dtype=jnp.int32)
    slot = at_right // rows
    fsdp_left = (at_left // rows % NY * NZ + z) * NC + c
    fsdp_right = (y * NZ + slot % NZ) * NC + (c ^ slot // NZ)
    key_left = jnp.where(at_left // (rows * NY) == x, fsdp_left * rows + at_left % rows, -1).astype(F32)
    key_right = (fsdp_right * rows + at_right % rows).astype(F32)
    mate_left = jnp.where(jnp.arange(NX)[:, None] == x, mates.reshape(1, -1), -1.0).reshape(-1)
    diag = key_left[:, None] == key_right[None, :]
    hit = mate_left[:, None] == key_right[None, :]
    expd = jnp.where(diag, 0.0, jnp.exp(sim - 1.0 / TEMPER))
    spos = jnp.sum(jnp.where(hit, sim, 0.0))

    row_sum = jnp.sum(expd, axis=1).reshape(NX * NY, rows)
    col_sum = jnp.sum(expd, axis=0).reshape(NC, NZ, rows)
    col_sum = col_sum + swap(col_sum)[::-1]
    row_sum = jnp.sum(every(row_sum, ("x", "y"), NX * NY), axis=0)
    col_sum = jnp.sum(every(col_sum, "z", NZ), axis=0)
    lse = jnp.log(lax.dynamic_index_in_dim(row_sum, x * NY + y, 0, False)) + 1.0 / TEMPER
    loss = jnp.sum(lse) - spos

    weight = expd * ((1.0 / row_sum).reshape(-1)[:, None] + (1.0 / col_sum).reshape(-1)[None, :])
    weight = jnp.where(hit, weight - 2.0, weight).astype(BF)
    grad_emb = dot(weight, right).astype(BF).reshape(NX * NY, rows, width)
    grad_emb = jnp.sum(trade(grad_emb, ("x", "y")).astype(F32), axis=0) / TEMPER
    dproj = ((grad_emb - unit * jnp.sum(unit * grad_emb, axis=1, keepdims=True)) / norm[:, None]).astype(BF)

    dproj = jnp.concatenate(gather_x(dproj), axis=0)
    dact = dot_nt(dproj, second)
    dpre = jnp.where(pre > 0.0, dact, 0.0).astype(BF)
    wide = jnp.pad(dproj, ((0, 0), (0, part - width)))
    lane = jnp.arange(part, dtype=jnp.int32) == width

    def grads_of(feat, acts, mark, value):
        return dot(feat, value) + dot(acts, wide) + jnp.where(mark[:, None] & lane[None, :], loss, 0.0)

    grads, dpre = tie(grads_of(feat_b, act_b, mark_b, dpre).astype(BF), dpre)
    got = swap(grads)
    gfeat = dot_nt(dpre, first).astype(BF).reshape(NX, rows, depth)
    grads = grads_of(feat_a, act_a, mark_a, dpre)
    gfeat, grads = tie(gfeat, grads)
    grads = (grads + got.astype(F32)).astype(BF).reshape(NZ, block, part)
    moved = [flip_x(gfeat[j], j) for j in range(1, NX)]
    grads = jnp.sum(trade(grads, "z").astype(F32), axis=0).reshape(NY + 1, pad, part)
    own, grads = tie(gfeat[0], grads)
    grads = jnp.concatenate([grads[:NY], jnp.broadcast_to(grads[NY:], (NY, pad, part))], axis=1)
    grads = jnp.sum(trade(grads, "y"), axis=0)
    gfeat = sum(moved, own.astype(F32)).astype(BF)
    grads = every(grads, "x", NX)
    count = jnp.float32(rows * NX * NY * NZ * NC)
    scale = 1.0 / jnp.sqrt(count)
    out_first = jnp.concatenate([grads[k, :share] for k in range(NX)], axis=1) * scale
    out_second = lax.dynamic_index_in_dim(grads, y, 0, False)[pad : pad + share, :width] * scale
    loss = jnp.sum(grads[:, pad, width]) / count
    return (loss, gfeat, out_first, out_second)


def solution(mesh):
    axes = ("x", "y", "z", "c")
    fsdp = axes[1:]
    return jax.shard_map(
        on_device,
        mesh=Mesh(mesh.devices.reshape(NX, NY, NZ, NC), axes),
        in_specs=(P(axes, None), P(fsdp, None), P(fsdp, None), P(axes)),
        out_specs=(P(), P(axes, None), P(fsdp, None), P(fsdp, None)),
        check_vma=False,
    )
```

```python
import functools

import jax
import jax.numpy as jnp
from jax import lax
from jax.experimental import pallas as pl
from jax.experimental.pallas import tpu as pltpu
from jax.sharding import Mesh, PartitionSpec as P

TEMPER = 0.1
EPSILON = 1e-06
NX, NY, NZ, NC = 4, 4, 8, 2
BF = jnp.bfloat16
F32 = jnp.float32


def swap(v):
    return lax.ppermute(v, "c", [(0, 1), (1, 0)])


def flip_x(v, j):
    return lax.ppermute(v, "x", [(i, i ^ j) for i in range(NX)])


def tie(*values):
    return lax.optimization_barrier(values)


def trade(v, axes):
    return lax.all_to_all(v, axes, 0, 0, tiled=True)


def every(v, axes, size):
    return trade(jnp.broadcast_to(v[None], (size,) + v.shape), axes)


def gather_in_order(v, axis, size):
    at = lax.axis_index(axis)
    out = lax.dynamic_update_slice_in_dim(jnp.zeros((size,) + v.shape, v.dtype), v[None], at, 0)
    for j in range(1, size):
        got = lax.ppermute(v, axis, [(i, i ^ j) for i in range(size)])
        out = lax.dynamic_update_slice_in_dim(out, got[None], at ^ j, 0)
    return out.reshape((size * v.shape[0],) + v.shape[1:])


def dot(a, b):
    return jnp.dot(a, b, preferred_element_type=F32)


def dot_nt(a, b):
    return lax.dot_general(a, b, (((1,), (1,)), ((), ())), preferred_element_type=F32)


LANES = 128


def similarity_kernel(x_ref, left_ref, right_ref, keys_ref, key_ref, expd_ref, row_ref, col_ref, pos_ref):
    step, size = pl.program_id(0), left_ref.shape[0]
    per_plane = keys_ref.shape[1] // size

    @pl.when(step == 0)
    def _():
        col_ref[...] = jnp.zeros_like(col_ref)
        pos_ref[...] = jnp.zeros_like(pos_ref)

    def run(masked):
        total = jnp.zeros((size, LANES), F32)
        if masked:
            at = pl.ds(pl.multiple_of(step % per_plane * size, size), size)
            own, mate = keys_ref[0, at, :], keys_ref[1, at, :]
        for start in range(0, right_ref.shape[0], 2 * LANES):
            both = dot_nt(left_ref[...], right_ref[start : start + 2 * LANES, :]) * (1.0 / TEMPER)
            for half in range(2):
                cols = slice(start + half * LANES, start + (half + 1) * LANES)
                sim = both[:, half * LANES : (half + 1) * LANES]
                expd = jnp.exp(sim - 1.0 / TEMPER)
                if masked:
                    key = key_ref[:, cols]
                    expd = jnp.where(own == key, 0.0, expd)
                    pos_ref[:, cols] += jnp.sum(jnp.where(mate == key, sim, 0.0).reshape(size // 8, 8, LANES), axis=0)
                total += expd
                col_ref[:, cols] += jnp.sum(expd.reshape(size // 8, 8, LANES), axis=0)
                expd_ref[:, cols] = expd.astype(BF)
        row_ref[0] = jnp.sum(total.T, axis=0, keepdims=True)

    mine = step // per_plane == x_ref[0]
    pl.when(mine)(functools.partial(run, True))
    pl.when(jnp.logical_not(mine))(functools.partial(run, False))


def similarity(x, left, right, keys, key, size):
    n_left, n_right = left.shape[0], right.shape[0]
    whole = lambda shape: pl.BlockSpec(shape, lambda i: (0,) * len(shape))
    return pl.pallas_call(
        similarity_kernel,
        grid=(n_left // size,),
        in_specs=[
            pl.BlockSpec(memory_space=pltpu.SMEM),
            pl.BlockSpec((size, left.shape[1]), lambda i: (i, 0)),
            whole(right.shape),
            whole(keys.shape),
            whole(key.shape),
        ],
        out_specs=[
            pl.BlockSpec((size, n_right), lambda i: (i, 0)),
            pl.BlockSpec((1, 1, size), lambda i: (i, 0, 0)),
            whole((8, n_right)),
            whole((8, n_right)),
        ],
        out_shape=[
            jax.ShapeDtypeStruct((n_left, n_right), BF),
            jax.ShapeDtypeStruct((n_left // size, 1, size), F32),
            jax.ShapeDtypeStruct((8, n_right), F32),
            jax.ShapeDtypeStruct((8, n_right), F32),
        ],
        compiler_params=pltpu.CompilerParams(vmem_limit_bytes=40 * 2**20),
    )(x, left, right, keys, key)


def weighted_kernel(x_ref, expd_ref, right_ref, keys_ref, key_ref, row_ref, col_ref, out_ref, weight_ref):
    step, size = pl.program_id(0), expd_ref.shape[0]
    per_plane = keys_ref.shape[1] // size

    def run(masked):
        by_row = jnp.broadcast_to(1.0 / row_ref[0], (LANES, size)).T
        if masked:
            mate = keys_ref[1, pl.ds(pl.multiple_of(step % per_plane * size, size), size), :]
        for start in range(0, right_ref.shape[0], LANES):
            cols = slice(start, start + LANES)
            weight = expd_ref[:, cols].astype(F32) * (by_row + 1.0 / col_ref[:, cols])
            if masked:
                weight = jnp.where(mate == key_ref[:, cols], weight - 2.0, weight)
            weight_ref[:, cols] = weight.astype(BF)
        out_ref[...] = dot(weight_ref[...], right_ref[...]).astype(out_ref.dtype)

    mine = step // per_plane == x_ref[0]
    pl.when(mine)(functools.partial(run, True))
    pl.when(jnp.logical_not(mine))(functools.partial(run, False))


def weighted(x, expd, right, keys, key, row_sum, col_sum, size):
    n_left, n_right = expd.shape
    whole = lambda shape: pl.BlockSpec(shape, lambda i: (0,) * len(shape))
    return pl.pallas_call(
        weighted_kernel,
        grid=(n_left // size,),
        in_specs=[
            pl.BlockSpec(memory_space=pltpu.SMEM),
            pl.BlockSpec((size, n_right), lambda i: (i, 0)),
            whole(right.shape),
            whole(keys.shape),
            whole(key.shape),
            pl.BlockSpec((1, 1, size), lambda i: (i, 0, 0)),
            whole(col_sum.shape),
        ],
        out_specs=pl.BlockSpec((size, right.shape[1]), lambda i: (i, 0)),
        out_shape=jax.ShapeDtypeStruct((n_left, right.shape[1]), BF),
        scratch_shapes=[pltpu.VMEM((size, n_right), BF)],
        compiler_params=pltpu.CompilerParams(vmem_limit_bytes=40 * 2**20),
    )(x, expd, right, keys, key, row_sum, col_sum)


def on_device(features, w_first, w_second, partner):
    rows, depth = features.shape
    hidden, width = w_second.shape[0] * NY * NZ * NC, w_second.shape[1]
    share = depth // (NY * NZ * NC)
    pad = -(-share // 8) * 8
    part = hidden // NX
    block = (NY + 1) * pad
    x, y, z, c = (lax.axis_index(name) for name in "xyzc")

    first = sum(jnp.where(x == k, w_first[:, k * part : (k + 1) * part], 0) for k in range(NX))
    first = jnp.pad(first, ((0, pad - share), (0, 0)))
    second = jnp.pad(w_second, ((0, pad - share), (0, part - width)))
    local = partner % (rows * NY * NZ * NC)
    marks = jnp.concatenate([local // rows, local % rows]).astype(BF)[None, :]
    marks = jnp.pad(marks, ((0, 7), (0, part - 2 * rows)))
    near = every(jnp.concatenate([first, second, marks], axis=0), "y", NY)
    mates = near[:, 2 * pad, :rows].astype(F32) * rows + near[:, 2 * pad, rows : 2 * rows].astype(F32)
    chosen = lax.dynamic_index_in_dim(near, x, 0, False)[pad : 2 * pad]

    half_a = every(jnp.concatenate([near[k, :pad] for k in range(NY)] + [chosen], axis=0), "z", NZ)
    half_a = half_a.reshape(NZ * block, part)
    half_b = swap(half_a)

    def places(flip):
        col = jnp.arange(NZ * block, dtype=jnp.int32)
        line, kind = col % pad, col % block // pad
        slot = col // block * NC + (c ^ flip)
        row = jnp.where(kind < NY, (kind * (NZ * NC) + slot) * share, depth + slot * share) + line
        row = jnp.where(line < share, row, -1)
        spread = (jnp.arange(depth + part, dtype=jnp.int32)[:, None] == row[None, :]).astype(BF)
        return spread, (kind == NY) & (line == 0)

    (spread_a, mark_a), (spread_b, mark_b) = places(0), places(1)
    feats = gather_in_order(features, "x", NX)

    whole, half_b = tie(dot(spread_a, half_a), half_b)
    whole = (whole + dot(spread_b, half_b)).astype(BF)
    first, second = whole[:depth], whole[depth:, :width]
    pre = dot(feats, first)
    act = jnp.maximum(pre, 0.0).astype(BF)
    proj = dot(act, second).reshape(NX, rows, width)
    proj = sum(flip_x(lax.dynamic_index_in_dim(proj, x ^ j, 0, False), j) for j in range(1, NX)) + lax.dynamic_index_in_dim(proj, x, 0, False)
    norm = jnp.sqrt(jnp.sum(proj * proj, axis=1) + EPSILON)
    unit = proj / norm[:, None]
    emb = unit.astype(BF)

    def turned(spread, value):
        return lax.dot_general(spread, value, (((0,), (1,)), ((), ())), preferred_element_type=F32).astype(BF)

    _, late_feats, late_act = tie(emb, feats, act)
    later = [turned(s[:depth], late_feats) for s in (spread_a, spread_b)]
    later += [turned(s[depth:], late_act) for s in (spread_a, spread_b)]
    right = every(emb, "z", NZ).reshape(NZ * rows, width)
    right, (feat_a, feat_b, act_a, act_b) = tie(right, later)
    right = jnp.concatenate([right, swap(right)], axis=0)
    left = gather_in_order(gather_in_order(emb, "y", NY), "x", NX)
    size = min(2 * rows, 256)
    slot = jnp.arange(NC * NZ * rows, dtype=jnp.int32) // rows
    line = jnp.arange(NC * NZ * rows, dtype=jnp.int32) % rows
    key = ((y * NZ + slot % NZ) * NC + (c ^ slot // NZ)) * rows + line
    own = ((slot[: NY * rows] * NZ + z) * NC + c) * rows + line[: NY * rows]
    keys = jnp.stack([own.astype(F32), mates.reshape(-1)])
    keys = jnp.broadcast_to(keys[:, :, None], keys.shape + (LANES,))
    key = key.astype(F32)[None, :]
    plane = x.astype(jnp.int32)[None]
    expd, row_sum, col_sum, spos = similarity(plane, left, right, keys, key, size)

    row_sum = row_sum.reshape(NX * NY, rows)
    col_sum = jnp.sum(col_sum, axis=0).reshape(NC, NZ, rows)
    row_sum = jnp.sum(every(row_sum, ("x", "y"), NX * NY), axis=0)
    col_sum = col_sum + swap(col_sum)[::-1]
    low = col_sum + lax.ppermute(col_sum, "z", [(i, (i + 1) % NZ) for i in range(NZ)])
    wide = low + lax.ppermute(col_sum, "z", [(i, (i - 1) % NZ) for i in range(NZ)])
    col_sum = wide + lax.ppermute(wide, "z", [(i, (i + 3) % NZ) for i in range(NZ)])
    col_sum = col_sum + lax.ppermute(low, "z", [(i, (i - 3) % NZ) for i in range(NZ)])
    lse = jnp.log(lax.dynamic_index_in_dim(row_sum, x * NY + y, 0, False)) + 1.0 / TEMPER
    loss = jnp.sum(lse) - jnp.sum(spos)

    grad_emb = weighted(plane, expd, right, keys, key, row_sum.reshape(-1, 1, size), col_sum.reshape(1, -1), size)
    grad_emb = trade(grad_emb.reshape(NX * NY, rows, width), ("x", "y"))
    grad_emb = jnp.sum(grad_emb.astype(F32), axis=0) / TEMPER
    dproj = ((grad_emb - unit * jnp.sum(unit * grad_emb, axis=1, keepdims=True)) / norm[:, None]).astype(BF)

    dproj = gather_in_order(dproj, "x", NX)
    dact = dot_nt(dproj, second)
    dpre = jnp.where(pre > 0.0, dact, 0.0).astype(BF)
    wide = jnp.pad(dproj, ((0, 0), (0, part - width)))
    lane = jnp.arange(part, dtype=jnp.int32) == width

    def grads_of(feat, acts, mark, value):
        return dot(feat, value) + dot(acts, wide) + jnp.where(mark[:, None] & lane[None, :], loss, 0.0)

    grads, dpre = tie(grads_of(feat_b, act_b, mark_b, dpre).astype(BF), dpre)
    got = swap(grads)
    gfeat = dot_nt(dpre, first).astype(BF).reshape(NX, rows, depth)
    grads = grads_of(feat_a, act_a, mark_a, dpre)
    gfeat, grads = tie(gfeat, grads)
    grads = (grads + got.astype(F32)).astype(BF).reshape(NZ, block, part)
    moved = [flip_x(lax.dynamic_index_in_dim(gfeat, x ^ j, 0, False), j) for j in range(1, NX)]
    grads = jnp.sum(trade(grads, "z").astype(F32), axis=0).reshape(NY + 1, pad, part)
    own, grads = tie(lax.dynamic_index_in_dim(gfeat, x, 0, False), grads)
    grads = jnp.concatenate([grads[:NY], jnp.broadcast_to(grads[NY:], (NY, pad, part))], axis=1)
    grads = jnp.sum(trade(grads, "y"), axis=0)
    gfeat = sum(moved, own.astype(F32)).astype(BF)
    grads = every(grads, "x", NX)
    count = jnp.float32(rows * NX * NY * NZ * NC)
    scale = 1.0 / jnp.sqrt(count)
    out_first = jnp.concatenate([grads[k, :share] for k in range(NX)], axis=1) * scale
    out_second = lax.dynamic_index_in_dim(grads, y, 0, False)[pad : pad + share, :width] * scale
    loss = jnp.sum(grads[:, pad, width]) / count
    return (loss, gfeat, out_first, out_second)


def solution(mesh):
    axes = ("x", "y", "z", "c")
    fsdp = axes[1:]
    return jax.shard_map(
        on_device,
        mesh=Mesh(mesh.devices.reshape(NX, NY, NZ, NC), axes),
        in_specs=(P(axes, None), P(fsdp, None), P(fsdp, None), P(axes)),
        out_specs=(P(), P(axes, None), P(fsdp, None), P(fsdp, None)),
        check_vma=False,
    )
```

```python
import functools
import math

import jax
import jax.numpy as jnp
from jax import lax
from jax.experimental import pallas as pl
from jax.experimental.pallas import tpu as pltpu
from jax.sharding import Mesh, PartitionSpec as P

TEMPER = 0.1
EPSILON = 1e-06
NX, NY, NZ, NC = 4, 4, 8, 2
BF = jnp.bfloat16
F32 = jnp.float32


def swap(v):
    return lax.ppermute(v, "c", [(0, 1), (1, 0)])


def flip_x(v, j):
    return lax.ppermute(v, "x", [(i, i ^ j) for i in range(NX)])


def tie(*values):
    return lax.optimization_barrier(values)


def trade(v, axes):
    return lax.all_to_all(v, axes, 0, 0, tiled=True)


def every(v, axes, size):
    return trade(jnp.broadcast_to(v[None], (size,) + v.shape), axes)


def dot(a, b):
    return jnp.dot(a, b, preferred_element_type=F32)


def dot_nt(a, b):
    return lax.dot_general(a, b, (((1,), (1,)), ((), ())), preferred_element_type=F32)


LANES, CHUNK = 128, 512
SCALE = math.log2(math.e) / TEMPER


def exp_similarity(left, right):
    sim = dot_nt(left, right)
    return sim, jnp.exp2(sim * SCALE - SCALE)


def similarity_kernel(x_ref, left_ref, right_ref, keys_ref, key_ref, row_ref, col_ref, pos_ref):
    size = left_ref.shape[0]

    @pl.when(pl.program_id(0) == 0)
    def _():
        col_ref[...] = jnp.zeros_like(col_ref)
        pos_ref[...] = jnp.zeros_like(pos_ref)

    def run(masked):
        total = jnp.zeros((size, LANES), F32)
        for start in range(0, right_ref.shape[0], CHUNK):
            sims, expds = exp_similarity(left_ref[...], right_ref[start : start + CHUNK, :])
            for at in range(0, CHUNK, LANES):
                cols = slice(start + at, start + at + LANES)
                sim, expd = sims[:, at : at + LANES], expds[:, at : at + LANES]
                if masked:
                    key = key_ref[:, cols]
                    expd = jnp.where(keys_ref[0] == key, 0.0, expd)
                    sim = jnp.where(keys_ref[1] == key, sim * (1.0 / TEMPER), 0.0)
                    pos_ref[:, cols] += jnp.sum(sim.reshape(size // 8, 8, LANES), axis=0)
                total += expd
                col_ref[:, cols] += jnp.sum(expd.reshape(size // 8, 8, LANES), axis=0)
        row_ref[0] = jnp.sum(total.T, axis=0, keepdims=True)

    mine = pl.program_id(0) == x_ref[0]
    pl.when(mine)(functools.partial(run, True))
    pl.when(jnp.logical_not(mine))(functools.partial(run, False))


def whole(array):
    return pl.BlockSpec(array.shape, lambda i: (0,) * array.ndim)


def similarity(x, left, right, keys, key):
    size, n_right = keys.shape[1], right.shape[0]
    steps = left.shape[0] // size
    parts = jax.ShapeDtypeStruct((8, n_right), F32)
    return pl.pallas_call(
        similarity_kernel,
        grid=(steps,),
        in_specs=[
            pl.BlockSpec(memory_space=pltpu.SMEM),
            pl.BlockSpec((size, left.shape[1]), lambda i: (i, 0)),
            whole(right),
            whole(keys),
            whole(key),
        ],
        out_specs=[pl.BlockSpec((1, 1, size), lambda i: (i, 0, 0)), whole(parts), whole(parts)],
        out_shape=[jax.ShapeDtypeStruct((steps, 1, size), F32), parts, parts],
        compiler_params=pltpu.CompilerParams(vmem_limit_bytes=32 * 2**20),
    )(x, left, right, keys, key)


def weighted_kernel(x_ref, left_ref, right_ref, keys_ref, key_ref, row_ref, col_ref, out_ref, weight_ref):
    size = left_ref.shape[0]

    def run(masked):
        by_row = jnp.broadcast_to(1.0 / row_ref[0], (LANES, size)).T
        for start in range(0, right_ref.shape[0], CHUNK):
            _, expds = exp_similarity(left_ref[...], right_ref[start : start + CHUNK, :])
            for at in range(0, CHUNK, LANES):
                cols = slice(start + at, start + at + LANES)
                weight = expds[:, at : at + LANES] * (by_row + 1.0 / col_ref[:, cols])
                if masked:
                    key = key_ref[:, cols]
                    weight = jnp.where(keys_ref[0] == key, 0.0, weight)
                    weight = jnp.where(keys_ref[1] == key, weight - 2.0, weight)
                weight_ref[:, cols] = weight.astype(BF)
        out_ref[...] = dot(weight_ref[...], right_ref[...]).astype(out_ref.dtype)

    mine = pl.program_id(0) == x_ref[0]
    pl.when(mine)(functools.partial(run, True))
    pl.when(jnp.logical_not(mine))(functools.partial(run, False))


def weighted(x, left, right, keys, key, row_sum, col_sum):
    size = keys.shape[1]
    return pl.pallas_call(
        weighted_kernel,
        grid=(left.shape[0] // size,),
        in_specs=[
            pl.BlockSpec(memory_space=pltpu.SMEM),
            pl.BlockSpec((size, left.shape[1]), lambda i: (i, 0)),
            whole(right),
            whole(keys),
            whole(key),
            pl.BlockSpec((1, 1, size), lambda i: (i, 0, 0)),
            whole(col_sum),
        ],
        out_specs=pl.BlockSpec((size, right.shape[1]), lambda i: (i, 0)),
        out_shape=jax.ShapeDtypeStruct(left.shape, BF),
        scratch_shapes=[pltpu.VMEM((size, right.shape[0]), BF)],
        compiler_params=pltpu.CompilerParams(vmem_limit_bytes=32 * 2**20),
    )(x, left, right, keys, key, row_sum, col_sum)


def on_device(features, w_first, w_second, partner):
    rows, depth = features.shape
    hidden, width = w_second.shape[0] * NY * NZ * NC, w_second.shape[1]
    share = depth // (NY * NZ * NC)
    pad = -(-share // 8) * 8
    part = hidden // NX
    block = (NY + 1) * pad
    x, y, z, c = (lax.axis_index(name) for name in "xyzc")

    first = sum(jnp.where(x == k, w_first[:, k * part : (k + 1) * part], 0) for k in range(NX))
    first = jnp.pad(first, ((0, pad - share), (0, 0)))
    second = jnp.pad(w_second, ((0, pad - share), (0, part - width)))
    local = partner % (rows * NY * NZ * NC)
    marks = jnp.concatenate([local // rows, local % rows]).astype(BF)[None, :]
    marks = jnp.pad(marks, ((0, 7), (0, part - 2 * rows)))
    near = every(jnp.concatenate([first, second, marks], axis=0), "y", NY)
    def places(flip):
        col = jnp.arange(NZ * block, dtype=jnp.int32)
        line, kind = col % pad, col % block // pad
        slot = col // block * NC + (c ^ flip)
        col_first = jnp.where((kind < NY) & (line < share), (kind * (NZ * NC) + slot) * share + line, -1)
        col_second = jnp.where((kind == NY) & (line < share), slot * share + line, -1)
        spread = (jnp.arange(depth, dtype=jnp.int32)[:, None] == col_first[None, :]).astype(BF)
        spread_hid = (jnp.arange(part, dtype=jnp.int32)[:, None] == col_second[None, :]).astype(BF)
        return spread, spread_hid, (kind == NY) & (line == 0)

    def turned(spread, value):
        return lax.dot_general(spread, value, (((0,), (1,)), ((), ())), preferred_element_type=F32).astype(BF)

    (spread_a, hid_a, mark_a), (spread_b, hid_b, mark_b) = places(0), places(1)
    feats = [features] + [flip_x(features, j) for j in range(1, NX)]
    near, spread_a, hid_a = tie(near, spread_a, hid_a)
    mates = near[:, 2 * pad, :rows].astype(F32) * rows + near[:, 2 * pad, rows : 2 * rows].astype(F32)
    chosen = lax.dynamic_index_in_dim(near, x, 0, False)[pad : 2 * pad]
    half_a = every(jnp.concatenate([near[k, :pad] for k in range(NY)] + [chosen], axis=0), "z", NZ)
    half_a, feats, spread_b, hid_b = tie(half_a, jnp.concatenate(feats, axis=0), spread_b, hid_b)
    half_a = half_a.reshape(NZ * block, part)
    half_b = swap(half_a)

    first, second, half_b = tie(dot(spread_a, half_a), dot(hid_a, half_a), half_b)
    first = (first + dot(spread_b, half_b)).astype(BF)
    second = (second + dot(hid_b, half_b))[:, :width].astype(BF)
    pre = dot(feats, first)
    act = jnp.maximum(pre, 0.0).astype(BF)
    proj = dot(act, second).reshape(NX, rows, width)
    proj = sum((flip_x(proj[j], j) for j in range(1, NX)), proj[0])
    norm = jnp.sqrt(jnp.sum(proj * proj, axis=1) + EPSILON)
    unit = proj / norm[:, None]
    emb = unit.astype(BF)

    _, late_feats, late_act = tie(emb, feats, act)
    right = every(emb, "z", NZ).reshape(NZ * rows, width)
    act_a, act_b, feat_a = turned(hid_a, late_act), turned(hid_b, late_act), turned(spread_a, late_feats)
    right, act_a, act_b, feat_a, late_emb, late_feats = tie(right, act_a, act_b, feat_a, emb, late_feats)
    right = jnp.concatenate([right, swap(right)], axis=0)
    left = every(late_emb, ("x", "y"), NX * NY).reshape(NX * NY * rows, width)
    left, feat_b = tie(left, turned(spread_b, late_feats))
    slot = jnp.arange(NC * NZ * rows, dtype=jnp.int32) // rows
    line = jnp.arange(NC * NZ * rows, dtype=jnp.int32) % rows
    key = ((y * NZ + slot % NZ) * NC + (c ^ slot // NZ)) * rows + line
    own = ((slot[: NY * rows] * NZ + z) * NC + c) * rows + line[: NY * rows]
    keys = jnp.stack([own.astype(F32), mates.reshape(-1)])
    keys = jnp.broadcast_to(keys[:, :, None], keys.shape + (LANES,))
    key = key.astype(F32)[None, :]
    plane = x.astype(jnp.int32)[None]
    row_sum, col_sum, spos = similarity(plane, left, right, keys, key)

    row_sum = row_sum.reshape(NX * NY, rows)
    col_sum = jnp.sum(col_sum, axis=0).reshape(NC, NZ, rows)
    row_sum = jnp.sum(every(row_sum, ("x", "y"), NX * NY), axis=0)
    col_sum = col_sum + swap(col_sum)[::-1]
    low = col_sum + lax.ppermute(col_sum, "z", [(i, (i + 1) % NZ) for i in range(NZ)])
    wide = low + lax.ppermute(col_sum, "z", [(i, (i - 1) % NZ) for i in range(NZ)])
    col_sum = wide + lax.ppermute(wide, "z", [(i, (i + 3) % NZ) for i in range(NZ)])
    col_sum = col_sum + lax.ppermute(low, "z", [(i, (i - 3) % NZ) for i in range(NZ)])
    lse = jnp.log(lax.dynamic_index_in_dim(row_sum, x * NY + y, 0, False)) + 1.0 / TEMPER
    loss = jnp.sum(lse) - jnp.sum(spos)

    grad_emb = weighted(plane, left, right, keys, key, row_sum.reshape(NX, 1, -1), col_sum.reshape(1, -1))
    grad_emb = trade(grad_emb.reshape(NX * NY, rows, width), ("x", "y"))
    grad_emb = jnp.sum(grad_emb.astype(F32), axis=0) / TEMPER
    dproj = ((grad_emb - unit * jnp.sum(unit * grad_emb, axis=1, keepdims=True)) / norm[:, None]).astype(BF)

    dproj = jnp.concatenate([dproj] + [flip_x(dproj, j) for j in range(1, NX)], axis=0)
    dact = dot_nt(dproj, second)
    dpre = jnp.where(pre > 0.0, dact, 0.0).astype(BF)
    wide = jnp.pad(dproj, ((0, 0), (0, part - width)))
    lane = jnp.arange(part, dtype=jnp.int32) == width

    def grads_of(feat, acts, mark, value):
        return dot(feat, value) + dot(acts, wide) + jnp.where(mark[:, None] & lane[None, :], loss, 0.0)

    grads, dpre = tie(grads_of(feat_b, act_b, mark_b, dpre).astype(BF), dpre)
    got = swap(grads)
    gfeat = dot_nt(dpre, first).astype(BF).reshape(NX, rows, depth)
    grads = grads_of(feat_a, act_a, mark_a, dpre)
    gfeat, grads = tie(gfeat, grads)
    grads = (grads + got.astype(F32)).astype(BF).reshape(NZ, block, part)
    moved = [flip_x(gfeat[j], j) for j in range(1, NX)]
    grads = jnp.sum(trade(grads, "z").astype(F32), axis=0).reshape(NY + 1, pad, part)
    own, grads = tie(gfeat[0], grads)
    grads = jnp.concatenate([grads[:NY], jnp.broadcast_to(grads[NY:], (NY, pad, part))], axis=1)
    grads = jnp.sum(trade(grads, "y"), axis=0)
    gfeat = sum(moved, own.astype(F32)).astype(BF)
    grads = every(grads, "x", NX)
    count = jnp.float32(rows * NX * NY * NZ * NC)
    scale = 1.0 / jnp.sqrt(count)
    out_first = jnp.concatenate([grads[k, :share] for k in range(NX)], axis=1) * scale
    out_second = lax.dynamic_index_in_dim(grads, y, 0, False)[pad : pad + share, :width] * scale
    loss = jnp.sum(grads[:, pad, width]) / count
    return (loss, gfeat, out_first, out_second)


def solution(mesh):
    axes = ("x", "y", "z", "c")
    fsdp = axes[1:]
    return jax.shard_map(
        on_device,
        mesh=Mesh(mesh.devices.reshape(NX, NY, NZ, NC), axes),
        in_specs=(P(axes, None), P(fsdp, None), P(fsdp, None), P(axes)),
        out_specs=(P(), P(axes, None), P(fsdp, None), P(fsdp, None)),
        check_vma=False,
    )
```

```python
import functools
import math

import jax
import jax.numpy as jnp
from jax import lax
from jax.experimental import pallas as pl
from jax.experimental.pallas import tpu as pltpu
from jax.sharding import Mesh, PartitionSpec as P

TEMPER = 0.1
EPSILON = 1e-06
NX, NY, NZ, NC = 4, 4, 8, 2
BF = jnp.bfloat16
F32 = jnp.float32


ZSLOTS = [(1, s, f) for s in range(4) for f in (0, 1)] + [(1, 4, 0)]
ZSLOTS += [(-1, s, f) for s in (1, 2, 3) for f in (1, 0)] + [(-1, 4, 1)]


def swap(v):
    return lax.ppermute(v, "c", [(0, 1), (1, 0)])


def flip_x(v, j):
    return lax.ppermute(v, "x", [(i, i ^ j) for i in range(NX)])


def tie(*values):
    return lax.optimization_barrier(values)


def trade(v, axes):
    return lax.all_to_all(v, axes, 0, 0, tiled=True)


def every(v, axes, size):
    return trade(jnp.broadcast_to(v[None], (size,) + v.shape), axes)


def ring(v):
    pairs = [(z * NC + c, (z + 1 - 2 * c) % NZ * NC + c) for z in range(NZ) for c in range(NC)]
    return lax.ppermute(v, ("z", "c"), pairs)


def gather_zc(v, beside):
    m, made = v.shape[0], []
    pieces = [jnp.concatenate([v, swap(v)], axis=0)]
    for step in range(1, 5):
        pieces.append(ring(pieces[-1] if step < 4 else pieces[-1][:m]))
        if step < 4:
            pieces[-1], extra = tie(pieces[-1], beside[step - 1]())
            made.append(extra)
    return jnp.concatenate(pieces + [swap(jnp.concatenate(pieces[1:], axis=0))], axis=0), made


def reorder(table, v):
    return jnp.sum(jnp.where(table[:, :, None], v[None], 0.0), axis=1)


def dot(a, b):
    return jnp.dot(a, b, preferred_element_type=F32)


def dot_nt(a, b):
    return lax.dot_general(a, b, (((1,), (1,)), ((), ())), preferred_element_type=F32)


LANES, CHUNK = 128, 512
SCALE = math.log2(math.e) / TEMPER


def exp_similarity(left, right):
    sim = dot_nt(left, right)
    return sim, jnp.exp2(sim * SCALE - SCALE)


def similarity_kernel(x_ref, left_ref, right_ref, keys_ref, key_ref, row_ref, col_ref, pos_ref):
    size = left_ref.shape[0]

    @pl.when(pl.program_id(0) == 0)
    def _():
        col_ref[...] = jnp.zeros_like(col_ref)
        pos_ref[...] = jnp.zeros_like(pos_ref)

    def run(masked):
        total = jnp.zeros((size, LANES), F32)
        for start in range(0, right_ref.shape[0], CHUNK):
            sims, expds = exp_similarity(left_ref[...], right_ref[start : start + CHUNK, :])
            for at in range(0, CHUNK, LANES):
                cols = slice(start + at, start + at + LANES)
                sim, expd = sims[:, at : at + LANES], expds[:, at : at + LANES]
                if masked:
                    key = key_ref[:, cols]
                    expd = jnp.where(keys_ref[0] == key, 0.0, expd)
                    sim = jnp.where(keys_ref[1] == key, sim * (1.0 / TEMPER), 0.0)
                    pos_ref[:, cols] += jnp.sum(sim.reshape(size // 8, 8, LANES), axis=0)
                total += expd
                col_ref[:, cols] += jnp.sum(expd.reshape(size // 8, 8, LANES), axis=0)
        row_ref[0] = jnp.sum(total.T, axis=0, keepdims=True)

    mine = pl.program_id(0) == x_ref[0]
    pl.when(mine)(functools.partial(run, True))
    pl.when(jnp.logical_not(mine))(functools.partial(run, False))


def whole(array):
    return pl.BlockSpec(array.shape, lambda i: (0,) * array.ndim)


def similarity(x, left, right, keys, key):
    size, n_right = keys.shape[1], right.shape[0]
    steps = left.shape[0] // size
    parts = jax.ShapeDtypeStruct((8, n_right), F32)
    return pl.pallas_call(
        similarity_kernel,
        grid=(steps,),
        in_specs=[
            pl.BlockSpec(memory_space=pltpu.SMEM),
            pl.BlockSpec((size, left.shape[1]), lambda i: (i, 0)),
            whole(right),
            whole(keys),
            whole(key),
        ],
        out_specs=[pl.BlockSpec((1, 1, size), lambda i: (i, 0, 0)), whole(parts), whole(parts)],
        out_shape=[jax.ShapeDtypeStruct((steps, 1, size), F32), parts, parts],
        compiler_params=pltpu.CompilerParams(vmem_limit_bytes=32 * 2**20),
    )(x, left, right, keys, key)


def weighted_kernel(x_ref, left_ref, right_ref, keys_ref, key_ref, row_ref, col_ref, out_ref, weight_ref):
    size = left_ref.shape[0]

    def run(masked):
        by_row = jnp.broadcast_to(1.0 / row_ref[0], (LANES, size)).T
        for start in range(0, right_ref.shape[0], CHUNK):
            _, expds = exp_similarity(left_ref[...], right_ref[start : start + CHUNK, :])
            for at in range(0, CHUNK, LANES):
                cols = slice(start + at, start + at + LANES)
                weight = expds[:, at : at + LANES] * (by_row + 1.0 / col_ref[:, cols])
                if masked:
                    key = key_ref[:, cols]
                    weight = jnp.where(keys_ref[0] == key, 0.0, weight)
                    weight = jnp.where(keys_ref[1] == key, weight - 2.0, weight)
                weight_ref[:, cols] = weight.astype(BF)
        out_ref[...] = dot(weight_ref[...], right_ref[...]).astype(out_ref.dtype)

    mine = pl.program_id(0) == x_ref[0]
    pl.when(mine)(functools.partial(run, True))
    pl.when(jnp.logical_not(mine))(functools.partial(run, False))


def weighted(x, left, right, keys, key, row_sum, col_sum):
    size = keys.shape[1]
    return pl.pallas_call(
        weighted_kernel,
        grid=(left.shape[0] // size,),
        in_specs=[
            pl.BlockSpec(memory_space=pltpu.SMEM),
            pl.BlockSpec((size, left.shape[1]), lambda i: (i, 0)),
            whole(right),
            whole(keys),
            whole(key),
            pl.BlockSpec((1, 1, size), lambda i: (i, 0, 0)),
            whole(col_sum),
        ],
        out_specs=pl.BlockSpec((size, right.shape[1]), lambda i: (i, 0)),
        out_shape=jax.ShapeDtypeStruct(left.shape, BF),
        scratch_shapes=[pltpu.VMEM((size, right.shape[0]), BF)],
        compiler_params=pltpu.CompilerParams(vmem_limit_bytes=32 * 2**20),
    )(x, left, right, keys, key, row_sum, col_sum)


def on_device(features, w_first, w_second, partner):
    rows, depth = features.shape
    hidden, width = w_second.shape[0] * NY * NZ * NC, w_second.shape[1]
    share = depth // (NY * NZ * NC)
    pad = -(-share // 8) * 8
    part = hidden // NX
    block = (NY + 1) * pad
    x, y, z, c = (lax.axis_index(name) for name in "xyzc")

    first = sum(jnp.where(x == k, w_first[:, k * part : (k + 1) * part], 0) for k in range(NX))
    first = jnp.pad(first, ((0, pad - share), (0, 0)))
    second = jnp.pad(w_second, ((0, pad - share), (0, part - width)))
    local = partner % (rows * NY * NZ * NC)
    marks = jnp.concatenate([local // rows, local % rows]).astype(BF)[None, :]
    marks = jnp.pad(marks, ((0, 7), (0, part - 2 * rows)))
    near = every(jnp.concatenate([first, second, marks], axis=0), "y", NY)
    def places(flip):
        col = jnp.arange(NZ * block, dtype=jnp.int32)
        line, kind = col % pad, col % block // pad
        slot = col // block * NC + (c ^ flip)
        col_first = jnp.where((kind < NY) & (line < share), (kind * (NZ * NC) + slot) * share + line, -1)
        col_second = jnp.where((kind == NY) & (line < share), slot * share + line, -1)
        spread = (jnp.arange(depth, dtype=jnp.int32)[:, None] == col_first[None, :]).astype(BF)
        spread_hid = (jnp.arange(part, dtype=jnp.int32)[:, None] == col_second[None, :]).astype(BF)
        return spread, spread_hid, (kind == NY) & (line == 0)

    def turned(spread, value):
        return lax.dot_general(spread, value, (((0,), (1,)), ((), ())), preferred_element_type=F32).astype(BF)

    (spread_a, hid_a, mark_a), (spread_b, hid_b, mark_b) = places(0), places(1)
    feats = [features] + [flip_x(features, j) for j in range(1, NX)]
    near, spread_a, hid_a = tie(near, spread_a, hid_a)
    mates = near[:, 2 * pad, :rows].astype(F32) * rows + near[:, 2 * pad, rows : 2 * rows].astype(F32)
    chosen = lax.dynamic_index_in_dim(near, x, 0, False)[pad : 2 * pad]
    half_a = every(jnp.concatenate([near[k, :pad] for k in range(NY)] + [chosen], axis=0), "z", NZ)
    half_a, feats, spread_b, hid_b = tie(half_a, jnp.concatenate(feats, axis=0), spread_b, hid_b)
    half_a = half_a.reshape(NZ * block, part)
    half_b = swap(half_a)

    first, second, half_b = tie(dot(spread_a, half_a), dot(hid_a, half_a), half_b)
    first = (first + dot(spread_b, half_b)).astype(BF)
    second = (second + dot(hid_b, half_b))[:, :width].astype(BF)
    pre = dot(feats, first)
    act = jnp.maximum(pre, 0.0).astype(BF)
    proj = dot(act, second).reshape(NX, rows, width)
    proj = sum((flip_x(proj[j], j) for j in range(1, NX)), proj[0])
    norm = jnp.sqrt(jnp.sum(proj * proj, axis=1) + EPSILON)
    unit = proj / norm[:, None]
    emb = unit.astype(BF)

    _, late_act = tie(emb, act)
    left = every(emb, ("x", "y"), NX * NY).reshape(NX * NY * rows, width)
    beside = (lambda: turned(hid_a, late_act), lambda: turned(hid_b, late_act), lambda: left)
    right, (act_a, act_b, left) = gather_zc(emb, beside)
    zslot = jnp.stack([(z - sign * dist * (1 - 2 * c)) % NZ * NC + (c ^ flip) for sign, dist, flip in ZSLOTS])
    ztable = zslot[None, :] == jnp.arange(NZ * NC, dtype=jnp.int32)[:, None]
    slot = jnp.arange(NC * NZ * rows, dtype=jnp.int32) // rows
    line = jnp.arange(NC * NZ * rows, dtype=jnp.int32) % rows
    key = (y * NZ * NC + jnp.repeat(zslot, rows)) * rows + line
    own = ((slot[: NY * rows] * NZ + z) * NC + c) * rows + line[: NY * rows]
    keys = jnp.stack([own.astype(F32), mates.reshape(-1)])
    keys = jnp.broadcast_to(keys[:, :, None], keys.shape + (LANES,))
    key = key.astype(F32)[None, :]
    plane = x.astype(jnp.int32)[None]
    row_sum, col_sum, spos = similarity(plane, left, right, keys, key)

    row_sum = row_sum.reshape(NX * NY, rows)
    col_sum = reorder(ztable, jnp.sum(col_sum, axis=0).reshape(NZ * NC, rows))
    row_sum = jnp.sum(every(row_sum, ("x", "y"), NX * NY), axis=0)
    col_sum = col_sum + swap(col_sum)
    low = col_sum + lax.ppermute(col_sum, "z", [(i, (i + 1) % NZ) for i in range(NZ)])
    wide = low + lax.ppermute(col_sum, "z", [(i, (i - 1) % NZ) for i in range(NZ)])
    col_sum = wide + lax.ppermute(wide, "z", [(i, (i + 3) % NZ) for i in range(NZ)])
    col_sum = col_sum + lax.ppermute(low, "z", [(i, (i - 3) % NZ) for i in range(NZ)])
    col_sum = reorder(ztable.T, col_sum)
    lse = jnp.log(lax.dynamic_index_in_dim(row_sum, x * NY + y, 0, False)) + 1.0 / TEMPER
    loss = jnp.sum(lse) - jnp.sum(spos)

    grad_emb = weighted(plane, left, right, keys, key, row_sum.reshape(NX, 1, -1), col_sum.reshape(1, -1))
    grad_emb, late_feats = tie(grad_emb, feats)
    grad_emb = trade(grad_emb.reshape(NX * NY, rows, width), ("x", "y"))
    grad_emb, feat_a, feat_b = tie(grad_emb, turned(spread_a, late_feats), turned(spread_b, late_feats))
    grad_emb = jnp.sum(grad_emb.astype(F32), axis=0) / TEMPER
    dproj = ((grad_emb - unit * jnp.sum(unit * grad_emb, axis=1, keepdims=True)) / norm[:, None]).astype(BF)

    dproj = jnp.concatenate([dproj] + [flip_x(dproj, j) for j in range(1, NX)], axis=0)
    dact = dot_nt(dproj, second)
    dpre = jnp.where(pre > 0.0, dact, 0.0).astype(BF)
    wide = jnp.pad(dproj, ((0, 0), (0, part - width)))
    lane = jnp.arange(part, dtype=jnp.int32) == width

    def grads_of(feat, acts, mark, value):
        return dot(feat, value) + dot(acts, wide) + jnp.where(mark[:, None] & lane[None, :], loss, 0.0)

    grads, dpre = tie(grads_of(feat_b, act_b, mark_b, dpre).astype(BF), dpre)
    got = swap(grads)
    gfeat = dot_nt(dpre, first).astype(BF).reshape(NX, rows, depth)
    grads = grads_of(feat_a, act_a, mark_a, dpre)
    gfeat, grads = tie(gfeat, grads)
    grads = (grads + got.astype(F32)).astype(BF).reshape(NZ, block, part)
    moved = [flip_x(gfeat[j], j) for j in range(1, NX)]
    grads = jnp.sum(trade(grads, "z").astype(F32), axis=0).reshape(NY + 1, pad, part)
    own, grads = tie(gfeat[0], grads)
    grads = jnp.concatenate([grads[:NY], jnp.broadcast_to(grads[NY:], (NY, pad, part))], axis=1)
    grads = jnp.sum(trade(grads, "y"), axis=0)
    gfeat = sum(moved, own.astype(F32)).astype(BF)
    grads = every(grads, "x", NX)
    count = jnp.float32(rows * NX * NY * NZ * NC)
    scale = 1.0 / jnp.sqrt(count)
    out_first = jnp.concatenate([grads[k, :share] for k in range(NX)], axis=1) * scale
    out_second = lax.dynamic_index_in_dim(grads, y, 0, False)[pad : pad + share, :width] * scale
    loss = jnp.sum(grads[:, pad, width]) / count
    return (loss, gfeat, out_first, out_second)


def solution(mesh):
    axes = ("x", "y", "z", "c")
    fsdp = axes[1:]
    return jax.shard_map(
        on_device,
        mesh=Mesh(mesh.devices.reshape(NX, NY, NZ, NC), axes),
        in_specs=(P(axes, None), P(fsdp, None), P(fsdp, None), P(axes)),
        out_specs=(P(), P(axes, None), P(fsdp, None), P(fsdp, None)),
        check_vma=False,
    )
```

```python
import functools
import math

import jax
import jax.numpy as jnp
from jax import lax
from jax.experimental import pallas as pl
from jax.experimental.pallas import tpu as pltpu
from jax.sharding import Mesh, PartitionSpec as P

TEMPER = 0.1
EPSILON = 1e-06
NX, NY, NZ, NC = 4, 4, 8, 2
BF = jnp.bfloat16
F32 = jnp.float32


ZSLOTS = [(1, s, f) for s in range(4) for f in (0, 1)] + [(1, 4, 0)]
ZSLOTS += [(-1, s, f) for s in (1, 2, 3) for f in (1, 0)] + [(-1, 4, 1)]


def swap(v):
    return lax.ppermute(v, "c", [(0, 1), (1, 0)])


def flip_x(v, j):
    return lax.ppermute(v, "x", [(i, i ^ j) for i in range(NX)])


def tie(*values):
    return lax.optimization_barrier(values)


def trade(v, axes):
    return lax.all_to_all(v, axes, 0, 0, tiled=True)


def every(v, axes, size):
    return trade(jnp.broadcast_to(v[None], (size,) + v.shape), axes)


def ring(v):
    pairs = [(z * NC + c, (z + 1 - 2 * c) % NZ * NC + c) for z in range(NZ) for c in range(NC)]
    return lax.ppermute(v, ("z", "c"), pairs)


def gather_zc(v, beside):
    m, made = v.shape[0], []
    pieces = [jnp.concatenate([v, swap(v)], axis=0)]
    for step in range(1, 5):
        pieces.append(ring(pieces[-1] if step < 4 else pieces[-1][:m]))
        if step < 4:
            pieces[-1], extra = tie(pieces[-1], beside[step - 1]())
            made.append(extra)
    return jnp.concatenate(pieces + [swap(jnp.concatenate(pieces[1:], axis=0))], axis=0), made


def reorder(table, v):
    return jnp.sum(jnp.where(table[:, :, None], v[None], 0.0), axis=1)


def dot(a, b):
    return jnp.dot(a, b, preferred_element_type=F32)


def dot_nt(a, b):
    return lax.dot_general(a, b, (((1,), (1,)), ((), ())), preferred_element_type=F32)


LANES, CHUNK = 128, 512
SCALE = math.log2(math.e) / TEMPER


def exp_similarity(left, right):
    sim = dot_nt(left, right)
    return sim, jnp.exp2(sim * SCALE - SCALE)


def similarity_kernel(x_ref, left_ref, right_ref, keys_ref, key_ref, row_ref, col_ref, pos_ref):
    size = left_ref.shape[0]

    @pl.when(pl.program_id(0) == 0)
    def _():
        col_ref[...] = jnp.zeros_like(col_ref)
        pos_ref[...] = jnp.zeros_like(pos_ref)

    def run(masked):
        total = jnp.zeros((size, LANES), F32)
        for start in range(0, right_ref.shape[0], CHUNK):
            sims, expds = exp_similarity(left_ref[...], right_ref[start : start + CHUNK, :])
            for at in range(0, CHUNK, LANES):
                cols = slice(start + at, start + at + LANES)
                sim, expd = sims[:, at : at + LANES], expds[:, at : at + LANES]
                if masked:
                    key = key_ref[:, cols]
                    expd = jnp.where(keys_ref[0] == key, 0.0, expd)
                    sim = jnp.where(keys_ref[1] == key, sim * (1.0 / TEMPER), 0.0)
                    pos_ref[:, cols] += jnp.sum(sim.reshape(size // 8, 8, LANES), axis=0)
                total += expd
                col_ref[:, cols] += jnp.sum(expd.reshape(size // 8, 8, LANES), axis=0)
        row_ref[0] = jnp.sum(total.T, axis=0, keepdims=True)

    mine = pl.program_id(0) == x_ref[0]
    pl.when(mine)(functools.partial(run, True))
    pl.when(jnp.logical_not(mine))(functools.partial(run, False))


def whole(array):
    return pl.BlockSpec(array.shape, lambda i: (0,) * array.ndim)


def similarity(x, left, right, keys, key):
    size, n_right = keys.shape[1], right.shape[0]
    steps = left.shape[0] // size
    parts = jax.ShapeDtypeStruct((8, n_right), F32)
    return pl.pallas_call(
        similarity_kernel,
        grid=(steps,),
        in_specs=[
            pl.BlockSpec(memory_space=pltpu.SMEM),
            pl.BlockSpec((size, left.shape[1]), lambda i: (i, 0)),
            whole(right),
            whole(keys),
            whole(key),
        ],
        out_specs=[pl.BlockSpec((1, 1, size), lambda i: (i, 0, 0)), whole(parts), whole(parts)],
        out_shape=[jax.ShapeDtypeStruct((steps, 1, size), F32), parts, parts],
        compiler_params=pltpu.CompilerParams(vmem_limit_bytes=32 * 2**20),
    )(x, left, right, keys, key)


def weighted_kernel(x_ref, left_ref, right_ref, keys_ref, key_ref, row_ref, col_ref, out_ref, weight_ref):
    size = left_ref.shape[0]

    def run(masked):
        by_row = jnp.broadcast_to(1.0 / row_ref[0], (LANES, size)).T
        for start in range(0, right_ref.shape[0], CHUNK):
            _, expds = exp_similarity(left_ref[...], right_ref[start : start + CHUNK, :])
            for at in range(0, CHUNK, LANES):
                cols = slice(start + at, start + at + LANES)
                weight = expds[:, at : at + LANES] * (by_row + 1.0 / col_ref[:, cols])
                if masked:
                    key = key_ref[:, cols]
                    weight = jnp.where(keys_ref[0] == key, 0.0, weight)
                    weight = jnp.where(keys_ref[1] == key, weight - 2.0, weight)
                weight_ref[:, cols] = weight.astype(BF)
        out_ref[...] = dot(weight_ref[...], right_ref[...]).astype(out_ref.dtype)

    mine = pl.program_id(0) == x_ref[0]
    pl.when(mine)(functools.partial(run, True))
    pl.when(jnp.logical_not(mine))(functools.partial(run, False))


def weighted(x, left, right, keys, key, row_sum, col_sum):
    size = keys.shape[1]
    return pl.pallas_call(
        weighted_kernel,
        grid=(left.shape[0] // size,),
        in_specs=[
            pl.BlockSpec(memory_space=pltpu.SMEM),
            pl.BlockSpec((size, left.shape[1]), lambda i: (i, 0)),
            whole(right),
            whole(keys),
            whole(key),
            pl.BlockSpec((1, 1, size), lambda i: (i, 0, 0)),
            whole(col_sum),
        ],
        out_specs=pl.BlockSpec((size, right.shape[1]), lambda i: (i, 0)),
        out_shape=jax.ShapeDtypeStruct(left.shape, BF),
        scratch_shapes=[pltpu.VMEM((size, right.shape[0]), BF)],
        compiler_params=pltpu.CompilerParams(vmem_limit_bytes=32 * 2**20),
    )(x, left, right, keys, key, row_sum, col_sum)


def on_device(features, w_first, w_second, partner):
    rows, depth = features.shape
    hidden, width = w_second.shape[0] * NY * NZ * NC, w_second.shape[1]
    share = depth // (NY * NZ * NC)
    pad = -(-share // 8) * 8
    part = hidden // NX
    block = (NY + 1) * pad
    x, y, z, c = (lax.axis_index(name) for name in "xyzc")

    first = sum(jnp.where(x == k, w_first[:, k * part : (k + 1) * part], 0) for k in range(NX))
    first = jnp.pad(first, ((0, pad - share), (0, 0)))
    second = jnp.pad(w_second, ((0, pad - share), (0, part - width)))
    local = partner % (rows * NY * NZ * NC)
    marks = jnp.concatenate([local // rows, local % rows]).astype(BF)[None, :]
    marks = jnp.pad(marks, ((0, 7), (0, part - 2 * rows)))
    near = every(jnp.concatenate([first, second, marks], axis=0), "y", NY)
    def places(flip):
        col = jnp.arange(NZ * block, dtype=jnp.int32)
        line, kind = col % pad, col % block // pad
        slot = col // block * NC + (c ^ flip)
        col_first = jnp.where((kind < NY) & (line < share), (kind * (NZ * NC) + slot) * share + line, -1)
        col_second = jnp.where((kind == NY) & (line < share), slot * share + line, -1)
        spread = (jnp.arange(depth, dtype=jnp.int32)[:, None] == col_first[None, :]).astype(BF)
        spread_hid = (jnp.arange(part, dtype=jnp.int32)[:, None] == col_second[None, :]).astype(BF)
        return spread, spread_hid, (kind == NY) & (line == 0)

    def turned(spread, value):
        return lax.dot_general(spread, value, (((0,), (1,)), ((), ())), preferred_element_type=F32).astype(BF)

    (spread_a, hid_a, mark_a), (spread_b, hid_b, mark_b) = places(0), places(1)
    feats = [features, flip_x(features, 1)]
    near, spread_a, hid_a, features = tie(near, spread_a, hid_a, features)
    feats += [flip_x(features, j) for j in range(2, NX)]
    mates = near[:, 2 * pad, :rows].astype(F32) * rows + near[:, 2 * pad, rows : 2 * rows].astype(F32)
    chosen = lax.dynamic_index_in_dim(near, x, 0, False)[pad : 2 * pad]
    half_a = every(jnp.concatenate([near[k, :pad] for k in range(NY)] + [chosen], axis=0), "z", NZ)
    half_a, feats, spread_b, hid_b = tie(half_a, jnp.concatenate(feats, axis=0), spread_b, hid_b)
    half_a = half_a.reshape(NZ * block, part)
    half_b = swap(half_a)

    first, second, half_b = tie(dot(spread_a, half_a), dot(hid_a, half_a), half_b)
    first = (first + dot(spread_b, half_b)).astype(BF)
    second = (second + dot(hid_b, half_b))[:, :width].astype(BF)
    pre = dot(feats, first)
    act = jnp.maximum(pre, 0.0).astype(BF)
    proj = dot(act, second).reshape(NX, rows, width)
    proj = sum((flip_x(proj[j], j) for j in range(1, NX)), proj[0])
    norm = jnp.sqrt(jnp.sum(proj * proj, axis=1) + EPSILON)
    unit = proj / norm[:, None]
    emb = unit.astype(BF)

    _, late_act = tie(emb, act)
    left = every(emb, ("x", "y"), NX * NY).reshape(NX * NY * rows, width)
    beside = (lambda: turned(hid_a, late_act), lambda: turned(hid_b, late_act), lambda: left)
    right, (act_a, act_b, left) = gather_zc(emb, beside)
    zslot = jnp.stack([(z - sign * dist * (1 - 2 * c)) % NZ * NC + (c ^ flip) for sign, dist, flip in ZSLOTS])
    ztable = zslot[None, :] == jnp.arange(NZ * NC, dtype=jnp.int32)[:, None]
    slot = jnp.arange(NC * NZ * rows, dtype=jnp.int32) // rows
    line = jnp.arange(NC * NZ * rows, dtype=jnp.int32) % rows
    key = (y * NZ * NC + jnp.repeat(zslot, rows)) * rows + line
    own = ((slot[: NY * rows] * NZ + z) * NC + c) * rows + line[: NY * rows]
    keys = jnp.stack([own.astype(F32), mates.reshape(-1)])
    keys = jnp.broadcast_to(keys[:, :, None], keys.shape + (LANES,))
    key = key.astype(F32)[None, :]
    plane = x.astype(jnp.int32)[None]
    row_sum, col_sum, spos = similarity(plane, left, right, keys, key)

    row_sum = row_sum.reshape(NX * NY, rows)
    col_sum = reorder(ztable, jnp.sum(col_sum, axis=0).reshape(NZ * NC, rows))
    row_sum = jnp.sum(every(row_sum, ("x", "y"), NX * NY), axis=0)
    col_sum = col_sum + swap(col_sum)
    low = col_sum + lax.ppermute(col_sum, "z", [(i, (i + 1) % NZ) for i in range(NZ)])
    wide = low + lax.ppermute(col_sum, "z", [(i, (i - 1) % NZ) for i in range(NZ)])
    col_sum = wide + lax.ppermute(wide, "z", [(i, (i + 3) % NZ) for i in range(NZ)])
    col_sum = col_sum + lax.ppermute(low, "z", [(i, (i - 3) % NZ) for i in range(NZ)])
    col_sum = reorder(ztable.T, col_sum)
    lse = jnp.log(lax.dynamic_index_in_dim(row_sum, x * NY + y, 0, False)) + 1.0 / TEMPER
    loss = jnp.sum(lse) - jnp.sum(spos)

    grad_emb = weighted(plane, left, right, keys, key, row_sum.reshape(NX, 1, -1), col_sum.reshape(1, -1))
    grad_emb, late_feats = tie(grad_emb, feats)
    grad_emb = trade(grad_emb.reshape(NX * NY, rows, width), ("x", "y"))
    grad_emb, feat_a, feat_b = tie(grad_emb, turned(spread_a, late_feats), turned(spread_b, late_feats))
    grad_emb = jnp.sum(grad_emb.astype(F32), axis=0) / TEMPER
    dproj = ((grad_emb - unit * jnp.sum(unit * grad_emb, axis=1, keepdims=True)) / norm[:, None]).astype(BF)

    dproj = jnp.concatenate([dproj] + [flip_x(dproj, j) for j in range(1, NX)], axis=0)
    dact = dot_nt(dproj, second)
    dpre = jnp.where(pre > 0.0, dact, 0.0).astype(BF)
    wide = jnp.pad(dproj, ((0, 0), (0, part - width)))
    lane = jnp.arange(part, dtype=jnp.int32) == width

    def grads_of(feat, acts, mark, value):
        return dot(feat, value) + dot(acts, wide) + jnp.where(mark[:, None] & lane[None, :], loss, 0.0)

    grads, dpre = tie(grads_of(feat_b, act_b, mark_b, dpre).astype(BF), dpre)
    got = swap(grads)
    gfeat = dot_nt(dpre, first).astype(BF).reshape(NX, rows, depth)
    grads = grads_of(feat_a, act_a, mark_a, dpre)
    gfeat, grads = tie(gfeat, grads)
    grads = (grads + got.astype(F32)).astype(BF).reshape(NZ, block, part)
    moved = [flip_x(gfeat[j], j) for j in range(1, NX)]
    grads = jnp.sum(trade(grads, "z").astype(F32), axis=0).reshape(NY + 1, pad, part)
    own, grads = tie(gfeat[0], grads)
    grads = jnp.concatenate([grads[:NY], jnp.broadcast_to(grads[NY:], (NY, pad, part))], axis=1)
    grads = jnp.sum(trade(grads, "y"), axis=0)
    gfeat = sum(moved, own.astype(F32)).astype(BF)
    grads = every(grads, "x", NX)
    count = jnp.float32(rows * NX * NY * NZ * NC)
    scale = 1.0 / jnp.sqrt(count)
    out_first = jnp.concatenate([grads[k, :share] for k in range(NX)], axis=1) * scale
    out_second = lax.dynamic_index_in_dim(grads, y, 0, False)[pad : pad + share, :width] * scale
    loss = jnp.sum(grads[:, pad, width]) / count
    return (loss, gfeat, out_first, out_second)


def solution(mesh):
    axes = ("x", "y", "z", "c")
    fsdp = axes[1:]
    return jax.shard_map(
        on_device,
        mesh=Mesh(mesh.devices.reshape(NX, NY, NZ, NC), axes),
        in_specs=(P(axes, None), P(fsdp, None), P(fsdp, None), P(axes)),
        out_specs=(P(), P(axes, None), P(fsdp, None), P(fsdp, None)),
        check_vma=False,
    )
```
